32 devices in a mesh: row: 4 (over x, core), col: 8 (over z, y).
Axes of the slice: x: 2, y: 2, z: 4, core: 2. Of those that a mesh axis runs over, the one named last changes fastest.
Arguments:
- strip_factors: bfloat16 [16384, 64], P(('row', 'col')), may hold values from -8 to 8
- sku_factors: bfloat16 [16384, 64], P('col', 'row'), may hold values from -8 to 8
- probe: bfloat16 [16384, 16], P('col', 'row'), may hold values from -6 to 6
- demand_weight: float32 [1, 16384], P(None, ('row', 'col')), may hold values from 1 to 30, as said below
Outputs:
- basis: float32 [16, 16384], P(None, ('row', 'col'))
The draws below stay inside these ranges and needn't reach their ends.
Inputs may be any that keep to these rules, and one draw needn't show every extreme that they name: `demand_weight`: positive weights.
All inputs are finite; a program needn't handle non-finite values.
Results may differ from the reference program's by a relative error of at most 0.009.
The reference program's roundings to bfloat16 on the way (of `strip_unit`, `sku_unit` and `affinity`) count: a program that leaves them out, or rounds other values in their place, can miss the bound.
Values may be sent and summed in bfloat16 or wider, within the bound.
A program may use at most 64 MiB of HBM per device.

```python
import jax
import jax.numpy as jnp
from jax import lax

K = 64
BLOCK = 16
C_BLK = 2048
STRIP = 16384
SKUS = 16384
N_COL = 8


cluster_count = 32


root_count = 4


def cluster_centres(key):
    root_rows = jnp.clip(jax.random.normal(jax.random.fold_in(key, 101), (root_count, K), jnp.float32), -4.0, 4.0)
    own_rows = jnp.clip(jax.random.normal(jax.random.fold_in(key, 102), (cluster_count, K), jnp.float32), -4.0, 4.0)
    parent = jnp.arange(cluster_count) % root_count
    return 0.8 * root_rows[parent] + 0.6 * own_rows


def member_rows(centres, key, jitter, spread_low, spread_high):
    row_count = jitter.shape[0]
    member_ids = jax.random.randint(jax.random.fold_in(key, 1), (row_count,), 0, cluster_count)
    sign_flip = (jax.random.randint(jax.random.fold_in(key, 2), (row_count, 1), 0, 2) * 2 - 1).astype(jnp.float32)
    spread = jnp.exp(jax.random.uniform(jax.random.fold_in(key, 3), (row_count, 1), jnp.float32, jnp.log(spread_low), jnp.log(spread_high)))
    return sign_flip * centres[member_ids] + spread * jitter


def draw_strip_factors(key, part):
    centres = cluster_centres(key)
    key = jax.random.fold_in(key, 5)
    jitter_key = jax.random.fold_in(key, 4)
    jitter = jnp.clip(jax.random.normal(jitter_key, (STRIP, K), jnp.float32), -4.0, 4.0)
    rows = member_rows(centres, key, jitter, 0.15, 0.6)
    return rows.astype(jnp.bfloat16)


def draw_sku_factors(key, part):
    centres = cluster_centres(key)
    key = jax.random.fold_in(key, 7)
    jitter_key = jax.random.fold_in(key, 4)
    jitter = jnp.clip(jax.random.normal(jitter_key, (SKUS, K), jnp.float32), -4.0, 4.0)
    rows = member_rows(centres, key, jitter, 0.15, 0.6)
    return rows.astype(jnp.bfloat16)


def draw_demand_weight(key, part):
    key = jax.random.fold_in(key, 11)
    place = jnp.arange(STRIP, dtype=jnp.float32) / STRIP
    ramp = jnp.exp(place * jnp.log(3.0))
    base = jnp.exp(jax.random.uniform(key, (1, STRIP), jnp.float32, 0.0, jnp.log(10.0)))
    return (base * ramp).astype(jnp.float32)


def block_scale(key, shape, shards, smallest, top_value):
    loudness, own = 1.0, jax.random.fold_in(key, 6)
    for dim, shards_of in shards:
        steps = jnp.exp(jax.random.uniform(jax.random.fold_in(own, dim), (shards_of,), jnp.float32, smallest / len(shards), top_value / len(shards)))
        loudness = loudness * jnp.repeat(steps, shape[dim] // shards_of).reshape([-1 if axis == dim else 1 for axis in range(len(shape))])
    return loudness


def bell_draw(key, dims, scale, most, pieces=(), kind=jnp.bfloat16):
    array = scale * jax.random.normal(key, dims, jnp.float32)
    if pieces:
        array = array * block_scale(key, dims, pieces, -0.22, 0.18)
    return jnp.clip(array, -most, most).astype(kind)


def setup_inputs(seed: int = 0) -> dict:
    splits = jax.random.split(jax.random.key(seed), 5)
    return {
        "strip_factors": draw_strip_factors(jax.random.fold_in(splits[4], 71), 0),
        "sku_factors": draw_sku_factors(jax.random.fold_in(splits[4], 71), 0),
        "probe": bell_draw(splits[2], (SKUS, BLOCK), 1.0, 6.0, ((0, 8), (1, 4))),
        "demand_weight": draw_demand_weight(jax.random.fold_in(splits[4], 71), 0),
    }


def unit_rows(factors):
    wide = factors.astype(jnp.float32)
    scale = lax.rsqrt(lax.optimization_barrier(jnp.sum(wide * wide, axis=1, keepdims=True)) + 1e-06)
    return (wide * scale).astype(jnp.bfloat16)

def reference(strip_factors, sku_factors, probe, demand_weight):
    strip_unit = unit_rows(strip_factors)
    sku_unit = unit_rows(sku_factors)
    panels = sku_unit.reshape(N_COL, C_BLK, K)
    probes = probe.reshape(N_COL, C_BLK, BLOCK)

    def add_block(total, pair):
        panel, columns = pair
        corr = jnp.dot(strip_unit.astype(jnp.float32), panel.T.astype(jnp.float32), preferred_element_type=jnp.float32)
        affinity = jnp.exp(corr).astype(jnp.bfloat16)
        return (total + jnp.dot(affinity.astype(jnp.float32), columns.astype(jnp.float32), preferred_element_type=jnp.float32).T, None)
    start = jnp.zeros((BLOCK, STRIP), jnp.float32)
    image, unused = lax.scan(add_block, start, (panels, probes))
    gram = jnp.dot(image * demand_weight, image.T, precision=lax.Precision.HIGHEST)
    lower = jnp.linalg.cholesky(gram)
    return jax.scipy.linalg.solve_triangular(lower, image, lower=True)
```

```python
import jax
import jax.numpy as jnp
from jax import lax
from jax.experimental import pallas as pl
from jax.experimental.pallas import tpu as pltpu
from jax.sharding import PartitionSpec as P

ROWS = 4
LINE = 4
GROUP = 2 * ROWS
CHUNK = 512


def unit_rows(factors):
    wide = factors.astype(jnp.float32)
    scale = lax.rsqrt(jnp.sum(wide * wide, axis=1, keepdims=True) + 1e-06)
    return (wide * scale).astype(jnp.bfloat16)


def per_device(strip_factors, sku_factors, probe, demand_weight):
    strip_unit = unit_rows(strip_factors)
    panel_raw, probe_cols = (
        lax.all_gather(sku_factors, "row", axis=1, tiled=True),
        lax.all_gather(probe, "row", axis=1, tiled=True),
    )
    sku_unit = unit_rows(panel_raw)
    columns = sku_unit.shape[0]
    width = min(512, columns)
    count = columns // width
    piece = lax.all_gather(strip_unit, "col", axis=0, tiled=True)
    total = jnp.zeros((probe_cols.shape[1], piece.shape[0]), jnp.float32)
    for number in range(count):
        panel = sku_unit[number * width : (number + 1) * width]
        block_probe = probe_cols[number * width : (number + 1) * width]
        corr = lax.dot_general(
            piece, panel, (((1,), (1,)), ((), ())), preferred_element_type=jnp.float32
        )
        affinity = jnp.exp(corr).astype(jnp.bfloat16)
        total = total + lax.dot_general(
            block_probe, affinity, (((0,), (1,)), ((), ())), preferred_element_type=jnp.float32
        )
    image = lax.psum_scatter(total, "col", scatter_dimension=1, tiled=True)
    local_gram = jnp.dot(image * demand_weight, image.T, precision=lax.Precision.HIGHEST)
    gram = lax.psum(local_gram, ("row", "col"))
    lower = jnp.linalg.cholesky(gram)
    return jax.scipy.linalg.solve_triangular(lower, image, lower=True)


def other(place, step):
    low = (place % 2 + step % 2) % 2
    high = (place // 2 + step // 2) % 2
    return 2 * high + low


def remote(source, target, sent, landed, row, col):
    return pltpu.make_async_remote_copy(
        src_ref=source,
        dst_ref=target,
        send_sem=sent,
        recv_sem=landed,
        device_id=(row, col),
        device_id_type=pl.DeviceIdType.MESH,
    )


def fused(
    strip_ref, sku_ref, probe_ref, weight_ref, out_ref,
    raw, probe_raw, probe_stage, probe_wide, full, units, strips, partial, arrived, gram_line, gram_group,
    sku_sent, sku_landed, probe_sent, probe_landed, strip_sent, strip_landed,
    pair_sent, pair_landed, twin_sent, twin_landed, image_sent, image_landed,
    line_sent, line_landed, group_sent, group_landed,
):
    row, col = lax.axis_index("row"), lax.axis_index("col")
    core = row % 2
    z, y = col // 2, col % 2
    twin = row + 1 - 2 * core
    mate = col + 1 - 2 * y
    part, skus = sku_ref.shape
    columns = probe_ref.shape[0]
    factors = ROWS * part
    block = ROWS * columns
    half = skus // 2
    fold = skus // ROWS

    def line_col(place):
        return place * 2 + y

    barrier = pltpu.get_barrier_semaphore()
    for step in range(1, ROWS):
        pl.semaphore_signal(barrier, inc=1, device_id=(other(row, step), col), device_id_type=pl.DeviceIdType.MESH)
    for step in range(1, LINE):
        pl.semaphore_signal(barrier, inc=1, device_id=(row, line_col(other(z, step))), device_id_type=pl.DeviceIdType.MESH)
    for step in range(ROWS):
        pl.semaphore_signal(barrier, inc=1, device_id=(other(row, step), mate), device_id_type=pl.DeviceIdType.MESH)

    raw[row] = sku_ref[...]
    for piece in range(ROWS):
        probe_stage[piece * columns : (piece + 1) * columns, :] = probe_ref[
            :, piece * fold : (piece + 1) * fold
        ].astype(jnp.float32)
    probe_raw[row] = probe_stage[...].astype(jnp.bfloat16)
    wide = strip_ref[...].astype(jnp.float32)
    scale = lax.rsqrt(jnp.sum(wide * wide, axis=0, keepdims=True) + 1e-06)
    strips[z] = (wide * scale).astype(jnp.bfloat16)

    pl.semaphore_wait(barrier, 2 * ROWS + LINE - 2)

    sends = []

    def send(copy):
        copy.start()
        sends.append(copy)

    for step in (2, 3, 1):
        there = other(row, step)
        send(remote(sku_ref, raw.at[row], sku_sent.at[step], sku_landed.at[row], there, col))
        send(remote(probe_raw.at[row], probe_raw.at[row], probe_sent.at[step], probe_landed.at[row], there, col))
    for step in range(1, LINE):
        there = line_col(other(z, step))
        send(remote(strips.at[z], strips.at[z], strip_sent.at[step], strip_landed.at[z], row, there))

    for step in range(1, ROWS):
        there = other(row, step)
        remote(sku_ref, raw.at[there], sku_sent.at[step], sku_landed.at[there], there, col).wait_recv()
        remote(
            probe_raw.at[there], probe_raw.at[there], probe_sent.at[step], probe_landed.at[there], there, col
        ).wait_recv()

    for there in range(ROWS):
        folded = probe_raw[there].astype(jnp.float32)
        for piece in range(ROWS):
            probe_wide[there * columns : (there + 1) * columns, piece * fold : (piece + 1) * fold] = folded[
                piece * columns : (piece + 1) * columns
            ]
    for side in range(2):
        lanes = slice(side * half, (side + 1) * half)
        wide = raw[:, :, lanes].reshape(factors, half).astype(jnp.float32)
        scale = lax.rsqrt(jnp.sum(wide * wide, axis=0, keepdims=True) + 1e-06)
        unit = (wide * scale).astype(jnp.bfloat16)
        full[0, side, 0:factors, :] = unit
        full[0, side, factors:, :] = probe_wide[:, lanes].astype(jnp.bfloat16)
        units[0, lanes, :] = unit.T

    pair = remote(full.at[0, core], full.at[1, core], pair_sent, pair_landed, row, mate)
    send(pair)
    relay = remote(full.at[1, core], full.at[1, core], twin_sent, twin_landed, twin, col)

    def image_block(which, place):
        strip = strips[place]
        total = jnp.zeros((block, strip.shape[1]), jnp.float32)
        for first in range(0, skus, CHUNK):
            corr = jnp.dot(units[which, first : first + CHUNK, :], strip, preferred_element_type=jnp.float32)
            affinity = jnp.exp(corr).astype(jnp.bfloat16)
            side, lane = first // half, first % half
            total = total + jnp.dot(
                full[which, side, factors:, lane : lane + CHUNK], affinity, preferred_element_type=jnp.float32
            )
        return total

    def own_half(step, carry):
        place = other(z, step)

        @pl.when(step > 0)
        def _():
            remote(
                strips.at[place], strips.at[place], strip_sent.at[step], strip_landed.at[place], row, line_col(place)
            ).wait_recv()

        partial[place] = image_block(0, place)

        @pl.when(step == 2)
        def _():
            pair.wait_recv()
            relay.start()

        return carry

    lax.fori_loop(0, LINE, own_half, 0)

    remote(full.at[1, 1 - core], full.at[1, 1 - core], twin_sent, twin_landed, twin, col).wait_recv()
    for side in range(2):
        units[1, side * half : (side + 1) * half, :] = full[1, side, 0:factors, :].T

    def mate_half(step, carry):
        place = other(z, LINE - 1 - step)
        partial[place] += image_block(1, place)

        @pl.when(step < LINE - 1)
        def _():
            remote(
                partial.at[place], arrived.at[z], image_sent.at[step], image_landed.at[z], row, line_col(place)
            ).start()

        return carry

    lax.fori_loop(0, LINE, mate_half, 0)

    image = partial[z]
    for step in range(1, LINE):
        place = other(z, step)
        remote(
            partial.at[place], arrived.at[place], image_sent.at[step], image_landed.at[place], row, line_col(place)
        ).wait_recv()
        image = image + arrived[place]

    local = lax.dot_general(
        image * weight_ref[...], image, (((1,), (1,)), ((), ())),
        precision=lax.Precision.HIGHEST, preferred_element_type=jnp.float32,
    )
    gram_line[z] = jnp.zeros(gram_line.shape[1:], jnp.float32)
    gram_line[z, :, 0:block] = local
    for step in range(1, LINE):
        there = line_col(other(z, step))
        send(remote(gram_line.at[z], gram_line.at[z], line_sent.at[step], line_landed.at[z], row, there))
    for step in range(1, LINE):
        place = other(z, step)
        remote(
            gram_line.at[place], gram_line.at[place], line_sent.at[step], line_landed.at[place], row, line_col(place)
        ).wait_recv()
    mine = row * 2 + y
    gram_group[mine] = (gram_line[0] + gram_line[1]) + (gram_line[2] + gram_line[3])
    for step in range(1, GROUP):
        there_row, there_y = other(row, step // 2), (y + step % 2) % 2
        send(
            remote(
                gram_group.at[mine], gram_group.at[mine], group_sent.at[step], group_landed.at[mine],
                there_row, z * 2 + there_y,
            )
        )
    for step in range(1, GROUP):
        there_row, there_y = other(row, step // 2), (y + step % 2) % 2
        slot = there_row * 2 + there_y
        remote(
            gram_group.at[slot], gram_group.at[slot], group_sent.at[step], group_landed.at[slot],
            there_row, z * 2 + there_y,
        ).wait_recv()
    gram = gram_group[0]
    for slot in range(1, GROUP):
        gram = gram + gram_group[slot]

    rank = lax.broadcasted_iota(jnp.int32, (block, 1), 0)
    diagonal = jnp.ones((block, 1), jnp.float32)
    basis = image
    for k in range(block):
        pivot = gram[k : k + 1, k : k + 1]
        diagonal = jnp.where(rank == k, pivot, diagonal)
        if k < block - 1:
            factor = jnp.where(rank > k, gram[:, k : k + 1] / pivot, 0.0)
            gram = gram - factor * gram[k : k + 1, :]
            basis = basis - factor * basis[k : k + 1, :]
    out_ref[...] = basis * lax.rsqrt(diagonal)

    for copy in sends:
        copy.wait_send()
    relay.wait_send()
    for step in range(LINE - 1):
        remote(partial.at[z], arrived.at[z], image_sent.at[step], image_landed.at[z], row, mate).wait_send()


def fused_per_device(strip_factors, sku_factors, probe, demand_weight):
    strip, factors = strip_factors.shape
    skus, part = sku_factors.shape
    columns = probe.shape[1]
    block = ROWS * columns
    bf16, f32 = jnp.bfloat16, jnp.float32
    dma = pltpu.SemaphoreType.DMA
    whole = pl.BlockSpec(memory_space=pltpu.VMEM)
    return pl.pallas_call(
        fused,
        out_shape=jax.ShapeDtypeStruct((block, strip), f32),
        in_specs=[whole] * 4,
        out_specs=whole,
        scratch_shapes=[
            pltpu.VMEM((ROWS, part, skus), bf16),
            pltpu.VMEM((ROWS, block, skus // ROWS), bf16),
            pltpu.VMEM((block, skus // ROWS), f32),
            pltpu.VMEM((block, skus), f32),
            pltpu.VMEM((2, 2, factors + block, skus // 2), bf16),
            pltpu.VMEM((2, skus, factors), bf16),
            pltpu.VMEM((LINE, factors, strip), bf16),
            pltpu.VMEM((LINE, block, strip), f32),
            pltpu.VMEM((LINE, block, strip), f32),
            pltpu.VMEM((LINE, block, 128), f32),
            pltpu.VMEM((GROUP, block, 128), f32),
        ]
        + [dma((ROWS,))] * 4 + [dma((LINE,))] * 2 + [dma] * 4 + [dma((LINE,))] * 4 + [dma((GROUP,))] * 2,
        compiler_params=pltpu.CompilerParams(
            collective_id=0, has_side_effects=True, vmem_limit_bytes=48 * 1024 * 1024
        ),
        cost_estimate=pl.CostEstimate(
            flops=2 * LINE * strip * 2 * skus * (factors + block),
            bytes_accessed=2 * (strip * factors + skus * part + skus * columns) + 4 * block * strip,
            transcendentals=LINE * strip * 2 * skus,
        ),
    )(strip_factors.T, sku_factors.T, probe.T, demand_weight)


def fits(mesh):
    return mesh.shape["row"] == ROWS and mesh.shape["col"] == 2 * LINE


def solution(mesh):
    placed = (P(("row", "col"), None), P("col", "row"), P("col", "row"), P(None, ("row", "col")))
    plan = fused_per_device if fits(mesh) else per_device
    return jax.shard_map(
        plan, mesh=mesh, in_specs=placed, out_specs=P(None, ("row", "col")), check_vma=False
    )
```

```python
import jax
import jax.numpy as jnp
from jax import lax
from jax.experimental import pallas as pl
from jax.experimental.pallas import tpu as pltpu
from jax.sharding import PartitionSpec as P

ROWS = 4
LINE = 4
GROUP = 2 * ROWS
CHUNK = 256


def unit_rows(factors):
    wide = factors.astype(jnp.float32)
    scale = lax.rsqrt(jnp.sum(wide * wide, axis=1, keepdims=True) + 1e-06)
    return (wide * scale).astype(jnp.bfloat16)


def per_device(strip_factors, sku_factors, probe, demand_weight):
    strip_unit = unit_rows(strip_factors)
    panel_raw, probe_cols = (
        lax.all_gather(sku_factors, "row", axis=1, tiled=True),
        lax.all_gather(probe, "row", axis=1, tiled=True),
    )
    sku_unit = unit_rows(panel_raw)
    columns = sku_unit.shape[0]
    width = min(512, columns)
    count = columns // width
    piece = lax.all_gather(strip_unit, "col", axis=0, tiled=True)
    total = jnp.zeros((probe_cols.shape[1], piece.shape[0]), jnp.float32)
    for number in range(count):
        panel = sku_unit[number * width : (number + 1) * width]
        block_probe = probe_cols[number * width : (number + 1) * width]
        corr = lax.dot_general(
            piece, panel, (((1,), (1,)), ((), ())), preferred_element_type=jnp.float32
        )
        affinity = jnp.exp(corr).astype(jnp.bfloat16)
        total = total + lax.dot_general(
            block_probe, affinity, (((0,), (1,)), ((), ())), preferred_element_type=jnp.float32
        )
    image = lax.psum_scatter(total, "col", scatter_dimension=1, tiled=True)
    local_gram = jnp.dot(image * demand_weight, image.T, precision=lax.Precision.HIGHEST)
    gram = lax.psum(local_gram, ("row", "col"))
    lower = jnp.linalg.cholesky(gram)
    return jax.scipy.linalg.solve_triangular(lower, image, lower=True)


def other(place, step):
    low = (place % 2 + step % 2) % 2
    high = (place // 2 + step // 2) % 2
    return 2 * high + low


def remote(source, target, sent, landed, row, col):
    return pltpu.make_async_remote_copy(
        src_ref=source,
        dst_ref=target,
        send_sem=sent,
        recv_sem=landed,
        device_id=(row, col),
        device_id_type=pl.DeviceIdType.MESH,
    )


def fused(
    strip_hbm, sku_ref, probe_hbm, weight_hbm, out_ref,
    strip_ref, probe_ref, weight_ref, raw, probe_raw, probe_stage, probe_wide, full, units, strips, partial, arrived, gram_line, gram_group,
    sku_sent, sku_landed, probe_sent, probe_landed, strip_sent, strip_landed,
    pair_sent, pair_landed, twin_sent, twin_landed, image_sent, image_landed,
    line_sent, line_landed, group_sent, group_landed, loaded,
):
    row, col = lax.axis_index("row"), lax.axis_index("col")
    core = row % 2
    z, y = col // 2, col % 2
    twin = row + 1 - 2 * core
    mate = col + 1 - 2 * y
    part, skus = sku_ref.shape
    columns = probe_ref.shape[0]
    loads = [
        pltpu.make_async_copy(source, target, loaded.at[number])
        for number, (source, target) in enumerate(
            ((strip_hbm, strip_ref), (probe_hbm, probe_ref), (weight_hbm, weight_ref), (sku_ref, raw.at[row]))
        )
    ]
    for load in loads:
        load.start()
    factors = ROWS * part
    block = ROWS * columns
    half = skus // 2
    fold = skus // ROWS

    def line_col(place):
        return place * 2 + y

    barrier = pltpu.get_barrier_semaphore()
    for step in range(1, ROWS):
        pl.semaphore_signal(barrier, inc=1, device_id=(other(row, step), col), device_id_type=pl.DeviceIdType.MESH)
    for step in range(1, LINE):
        pl.semaphore_signal(barrier, inc=1, device_id=(row, line_col(other(z, step))), device_id_type=pl.DeviceIdType.MESH)
    for step in range(ROWS):
        pl.semaphore_signal(barrier, inc=1, device_id=(other(row, step), mate), device_id_type=pl.DeviceIdType.MESH)

    loads[1].wait()
    for piece in range(ROWS):
        probe_stage[piece * columns : (piece + 1) * columns, :] = probe_ref[
            :, piece * fold : (piece + 1) * fold
        ].astype(jnp.float32)
    probe_raw[row] = probe_stage[...].astype(jnp.bfloat16)
    loads[0].wait()
    wide = strip_ref[...].astype(jnp.float32)
    scale = lax.rsqrt(jnp.sum(wide * wide, axis=0, keepdims=True) + 1e-06)
    strips[z] = (wide * scale).astype(jnp.bfloat16)

    pl.semaphore_wait(barrier, 2 * ROWS + LINE - 2)

    sends = []

    def send(copy):
        copy.start()
        sends.append(copy)

    for step in (2, 3, 1):
        there = other(row, step)
        send(remote(sku_ref, raw.at[row], sku_sent.at[step], sku_landed.at[row], there, col))
        send(remote(probe_raw.at[row], probe_raw.at[row], probe_sent.at[step], probe_landed.at[row], there, col))
    for step in range(1, LINE):
        there = line_col(other(z, step))
        send(remote(strips.at[z], strips.at[z], strip_sent.at[step], strip_landed.at[z], row, there))

    for step in range(1, ROWS):
        there = other(row, step)
        remote(sku_ref, raw.at[there], sku_sent.at[step], sku_landed.at[there], there, col).wait_recv()
        remote(
            probe_raw.at[there], probe_raw.at[there], probe_sent.at[step], probe_landed.at[there], there, col
        ).wait_recv()

    loads[3].wait()
    for there in range(ROWS):
        folded = probe_raw[there].astype(jnp.float32)
        for piece in range(ROWS):
            probe_wide[there * columns : (there + 1) * columns, piece * fold : (piece + 1) * fold] = folded[
                piece * columns : (piece + 1) * columns
            ]
    for side in range(2):
        lanes = slice(side * half, (side + 1) * half)
        wide = raw[:, :, lanes].reshape(factors, half).astype(jnp.float32)
        scale = lax.rsqrt(jnp.sum(wide * wide, axis=0, keepdims=True) + 1e-06)
        unit = (wide * scale).astype(jnp.bfloat16)
        full[0, side, 0:factors, :] = unit
        full[0, side, factors:, :] = probe_wide[:, lanes].astype(jnp.bfloat16)
        units[0, lanes, :] = unit.T

    pair = remote(full.at[0, core], full.at[1, core], pair_sent, pair_landed, row, mate)
    send(pair)
    relay = remote(full.at[1, core], full.at[1, core], twin_sent, twin_landed, twin, col)

    def image_block(which, place):
        totals = []
        for left in range(0, strips.shape[2], CHUNK):
            strip = strips[place, :, left : left + CHUNK]
            total = jnp.zeros((block, CHUNK), jnp.float32)
            for first in range(0, skus, CHUNK):
                corr = jnp.dot(units[which, first : first + CHUNK, :], strip, preferred_element_type=jnp.float32)
                affinity = jnp.exp(corr).astype(jnp.bfloat16)
                side, lane = first // half, first % half
                total = total + jnp.dot(
                    full[which, side, factors:, lane : lane + CHUNK], affinity, preferred_element_type=jnp.float32
                )
            totals.append(total)
        return jnp.concatenate(totals, axis=1)

    def own_half(step, carry):
        place = other(z, step)

        @pl.when(step > 0)
        def _():
            remote(
                strips.at[place], strips.at[place], strip_sent.at[step], strip_landed.at[place], row, line_col(place)
            ).wait_recv()

        partial[place] = image_block(0, place)

        @pl.when(step == 2)
        def _():
            pair.wait_recv()
            relay.start()

        return carry

    lax.fori_loop(0, LINE, own_half, 0)

    remote(full.at[1, 1 - core], full.at[1, 1 - core], twin_sent, twin_landed, twin, col).wait_recv()
    for side in range(2):
        units[1, side * half : (side + 1) * half, :] = full[1, side, 0:factors, :].T

    def mate_half(step, carry):
        place = other(z, LINE - 1 - step)
        partial[place] += image_block(1, place)

        @pl.when(step < LINE - 1)
        def _():
            remote(
                partial.at[place], arrived.at[z], image_sent.at[step], image_landed.at[z], row, line_col(place)
            ).start()

        return carry

    lax.fori_loop(0, LINE, mate_half, 0)

    image = partial[z]
    for step in range(1, LINE):
        place = other(z, step)
        remote(
            partial.at[place], arrived.at[place], image_sent.at[step], image_landed.at[place], row, line_col(place)
        ).wait_recv()
        image = image + arrived[place]

    loads[2].wait()
    local = lax.dot_general(
        image * weight_ref[...], image, (((1,), (1,)), ((), ())),
        precision=lax.Precision.HIGHEST, preferred_element_type=jnp.float32,
    )
    gram_line[z] = jnp.zeros(gram_line.shape[1:], jnp.float32)
    gram_line[z, :, 0:block] = local
    for step in range(1, LINE):
        there = line_col(other(z, step))
        send(remote(gram_line.at[z], gram_line.at[z], line_sent.at[step], line_landed.at[z], row, there))
    for step in range(1, LINE):
        place = other(z, step)
        remote(
            gram_line.at[place], gram_line.at[place], line_sent.at[step], line_landed.at[place], row, line_col(place)
        ).wait_recv()
    mine = row * 2 + y
    gram_group[mine] = (gram_line[0] + gram_line[1]) + (gram_line[2] + gram_line[3])
    for step in range(1, GROUP):
        there_row, there_y = other(row, step // 2), (y + step % 2) % 2
        send(
            remote(
                gram_group.at[mine], gram_group.at[mine], group_sent.at[step], group_landed.at[mine],
                there_row, z * 2 + there_y,
            )
        )
    for step in range(1, GROUP):
        there_row, there_y = other(row, step // 2), (y + step % 2) % 2
        slot = there_row * 2 + there_y
        remote(
            gram_group.at[slot], gram_group.at[slot], group_sent.at[step], group_landed.at[slot],
            there_row, z * 2 + there_y,
        ).wait_recv()
    gram = gram_group[0]
    for slot in range(1, GROUP):
        gram = gram + gram_group[slot]

    rank = lax.broadcasted_iota(jnp.int32, (block, 1), 0)
    diagonal = jnp.ones((block, 1), jnp.float32)
    basis = image
    for k in range(block):
        pivot = gram[k : k + 1, k : k + 1]
        diagonal = jnp.where(rank == k, pivot, diagonal)
        if k < block - 1:
            factor = jnp.where(rank > k, gram[:, k : k + 1] / pivot, 0.0)
            gram = gram - factor * gram[k : k + 1, :]
            basis = basis - factor * basis[k : k + 1, :]
    out_ref[...] = basis * lax.rsqrt(diagonal)

    for copy in sends:
        copy.wait_send()
    relay.wait_send()
    for step in range(LINE - 1):
        remote(partial.at[z], arrived.at[z], image_sent.at[step], image_landed.at[z], row, mate).wait_send()


def fused_per_device(strip_factors, sku_factors, probe, demand_weight):
    strip, factors = strip_factors.shape
    skus, part = sku_factors.shape
    columns = probe.shape[1]
    block = ROWS * columns
    bf16, f32 = jnp.bfloat16, jnp.float32
    dma = pltpu.SemaphoreType.DMA
    whole = pl.BlockSpec(memory_space=pltpu.VMEM)
    far = pl.BlockSpec(memory_space=pltpu.HBM)
    return pl.pallas_call(
        fused,
        out_shape=jax.ShapeDtypeStruct((block, strip), f32),
        in_specs=[far] * 4,
        out_specs=whole,
        scratch_shapes=[
            pltpu.VMEM((factors, strip), bf16),
            pltpu.VMEM((columns, skus), bf16),
            pltpu.VMEM((1, strip), f32),
            pltpu.VMEM((ROWS, part, skus), bf16),
            pltpu.VMEM((ROWS, block, skus // ROWS), bf16),
            pltpu.VMEM((block, skus // ROWS), f32),
            pltpu.VMEM((block, skus), f32),
            pltpu.VMEM((2, 2, factors + block, skus // 2), bf16),
            pltpu.VMEM((2, skus, factors), bf16),
            pltpu.VMEM((LINE, factors, strip), bf16),
            pltpu.VMEM((LINE, block, strip), f32),
            pltpu.VMEM((LINE, block, strip), f32),
            pltpu.VMEM((LINE, block, 128), f32),
            pltpu.VMEM((GROUP, block, 128), f32),
        ]
        + [dma((ROWS,))] * 4 + [dma((LINE,))] * 2 + [dma] * 4 + [dma((LINE,))] * 4 + [dma((GROUP,))] * 2 + [dma((4,))],
        compiler_params=pltpu.CompilerParams(
            collective_id=0, has_side_effects=True, vmem_limit_bytes=60 * 1024 * 1024
        ),
        cost_estimate=pl.CostEstimate(
            flops=2 * LINE * strip * 2 * skus * (factors + block),
            bytes_accessed=2 * (strip * factors + skus * part + skus * columns) + 4 * block * strip,
            transcendentals=LINE * strip * 2 * skus,
        ),
    )(strip_factors.T, sku_factors.T, probe.T, demand_weight)


def fits(mesh):
    return mesh.shape["row"] == ROWS and mesh.shape["col"] == 2 * LINE


def solution(mesh):
    placed = (P(("row", "col"), None), P("col", "row"), P("col", "row"), P(None, ("row", "col")))
    plan = fused_per_device if fits(mesh) else per_device
    return jax.shard_map(
        plan, mesh=mesh, in_specs=placed, out_specs=P(None, ("row", "col")), check_vma=False
    )
```

```python
import jax
import jax.numpy as jnp
from jax import lax
from jax.experimental import pallas as pl
from jax.experimental.pallas import tpu as pltpu
from jax.sharding import PartitionSpec as P

ROWS = 4
LINE = 4
GROUP = 2 * ROWS
CHUNK = 512


def unit_rows(factors):
    wide = factors.astype(jnp.float32)
    scale = lax.rsqrt(jnp.sum(wide * wide, axis=1, keepdims=True) + 1e-06)
    return (wide * scale).astype(jnp.bfloat16)


def per_device(strip_factors, sku_factors, probe, demand_weight):
    strip_unit = unit_rows(strip_factors)
    panel_raw, probe_cols = (
        lax.all_gather(sku_factors, "row", axis=1, tiled=True),
        lax.all_gather(probe, "row", axis=1, tiled=True),
    )
    sku_unit = unit_rows(panel_raw)
    columns = sku_unit.shape[0]
    width = min(512, columns)
    count = columns // width
    piece = lax.all_gather(strip_unit, "col", axis=0, tiled=True)
    total = jnp.zeros((probe_cols.shape[1], piece.shape[0]), jnp.float32)
    for number in range(count):
        panel = sku_unit[number * width : (number + 1) * width]
        block_probe = probe_cols[number * width : (number + 1) * width]
        corr = lax.dot_general(
            piece, panel, (((1,), (1,)), ((), ())), preferred_element_type=jnp.float32
        )
        affinity = jnp.exp(corr).astype(jnp.bfloat16)
        total = total + lax.dot_general(
            block_probe, affinity, (((0,), (1,)), ((), ())), preferred_element_type=jnp.float32
        )
    image = lax.psum_scatter(total, "col", scatter_dimension=1, tiled=True)
    local_gram = jnp.dot(image * demand_weight, image.T, precision=lax.Precision.HIGHEST)
    gram = lax.psum(local_gram, ("row", "col"))
    lower = jnp.linalg.cholesky(gram)
    return jax.scipy.linalg.solve_triangular(lower, image, lower=True)


def other(place, step):
    low = (place % 2 + step % 2) % 2
    high = (place // 2 + step // 2) % 2
    return 2 * high + low


def remote(source, target, sent, landed, row, col):
    return pltpu.make_async_remote_copy(
        src_ref=source,
        dst_ref=target,
        send_sem=sent,
        recv_sem=landed,
        device_id=(row, col),
        device_id_type=pl.DeviceIdType.MESH,
    )


def fused(
    strip_hbm, sku_ref, probe_hbm, weight_hbm, out_ref,
    strip_ref, probe_ref, weight_ref, raw, probe_raw, probe_stage, probe_wide, full, units, strips, partial, arrived, gram_line, gram_group,
    sku_sent, sku_landed, probe_sent, probe_landed, strip_sent, strip_landed,
    pair_sent, pair_landed, twin_sent, twin_landed, image_sent, image_landed,
    line_sent, line_landed, group_sent, group_landed, loaded,
):
    row, col = lax.axis_index("row"), lax.axis_index("col")
    core = row % 2
    z, y = col // 2, col % 2
    twin = row + 1 - 2 * core
    mate = col + 1 - 2 * y
    part, skus = sku_ref.shape
    columns = probe_ref.shape[0]
    loads = [
        pltpu.make_async_copy(source, target, loaded.at[number])
        for number, (source, target) in enumerate(
            ((strip_hbm, strip_ref), (probe_hbm, probe_ref), (weight_hbm, weight_ref), (sku_ref, raw.at[row]))
        )
    ]
    for load in loads:
        load.start()
    factors = ROWS * part
    block = ROWS * columns
    half = skus // 2
    fold = skus // ROWS

    def line_col(place):
        return place * 2 + y

    barrier = pltpu.get_barrier_semaphore()
    for step in range(1, ROWS):
        pl.semaphore_signal(barrier, inc=1, device_id=(other(row, step), col), device_id_type=pl.DeviceIdType.MESH)
    for step in range(1, LINE):
        pl.semaphore_signal(barrier, inc=1, device_id=(row, line_col(other(z, step))), device_id_type=pl.DeviceIdType.MESH)
    for step in range(ROWS):
        pl.semaphore_signal(barrier, inc=1, device_id=(other(row, step), mate), device_id_type=pl.DeviceIdType.MESH)

    loads[1].wait()
    for piece in range(ROWS):
        probe_stage[piece * columns : (piece + 1) * columns, :] = probe_ref[
            :, piece * fold : (piece + 1) * fold
        ].astype(jnp.float32)
    probe_raw[row] = probe_stage[...].astype(jnp.bfloat16)
    loads[0].wait()
    wide = strip_ref[...].astype(jnp.float32)
    scale = lax.rsqrt(jnp.sum(wide * wide, axis=0, keepdims=True) + 1e-06)
    strips[z] = (wide * scale).astype(jnp.bfloat16)

    pl.semaphore_wait(barrier, 2 * ROWS + LINE - 2)

    sends = []

    def send(copy):
        copy.start()
        sends.append(copy)

    for step in (2, 3, 1):
        there = other(row, step)
        send(remote(sku_ref, raw.at[row], sku_sent.at[step], sku_landed.at[row], there, col))
        send(remote(probe_raw.at[row], probe_raw.at[row], probe_sent.at[step], probe_landed.at[row], there, col))
    for step in range(1, LINE):
        there = line_col(other(z, step))
        send(remote(strips.at[z], strips.at[z], strip_sent.at[step], strip_landed.at[z], row, there))

    for step in range(1, ROWS):
        there = other(row, step)
        remote(sku_ref, raw.at[there], sku_sent.at[step], sku_landed.at[there], there, col).wait_recv()
        remote(
            probe_raw.at[there], probe_raw.at[there], probe_sent.at[step], probe_landed.at[there], there, col
        ).wait_recv()

    loads[3].wait()
    for there in range(ROWS):
        folded = probe_raw[there].astype(jnp.float32)
        for piece in range(ROWS):
            probe_wide[there * columns : (there + 1) * columns, piece * fold : (piece + 1) * fold] = folded[
                piece * columns : (piece + 1) * columns
            ]
    for side in range(2):
        lanes = slice(side * half, (side + 1) * half)
        wide = raw[:, :, lanes].reshape(factors, half).astype(jnp.float32)
        scale = lax.rsqrt(jnp.sum(wide * wide, axis=0, keepdims=True) + 1e-06)
        unit = (wide * scale).astype(jnp.bfloat16)
        full[0, side, 0:factors, :] = unit
        full[0, side, factors:, :] = probe_wide[:, lanes].astype(jnp.bfloat16)
        units[0, lanes, :] = unit.T

    pair = remote(full.at[0, core], full.at[1, core], pair_sent, pair_landed, row, mate)
    send(pair)
    relay = remote(full.at[1, core], full.at[1, core], twin_sent, twin_landed, twin, col)

    def image_block(which, place):
        totals = []
        for left in range(0, strips.shape[2], CHUNK):
            strip = strips[place, :, left : left + CHUNK]
            total = jnp.zeros((block, CHUNK), jnp.float32)
            for first in range(0, skus, CHUNK):
                corr = jnp.dot(units[which, first : first + CHUNK, :], strip, preferred_element_type=jnp.float32)
                affinity = jnp.exp(corr).astype(jnp.bfloat16)
                side, lane = first // half, first % half
                total = total + jnp.dot(
                    full[which, side, factors:, lane : lane + CHUNK], affinity, preferred_element_type=jnp.float32
                )
            totals.append(total)
        return jnp.concatenate(totals, axis=1)

    def own_half(step, carry):
        place = other(z, step)

        @pl.when(step > 0)
        def _():
            remote(
                strips.at[place], strips.at[place], strip_sent.at[step], strip_landed.at[place], row, line_col(place)
            ).wait_recv()

        partial[place] = image_block(0, place)

        @pl.when(step == 2)
        def _():
            pair.wait_recv()
            relay.start()

        return carry

    lax.fori_loop(0, LINE, own_half, 0)

    remote(full.at[1, 1 - core], full.at[1, 1 - core], twin_sent, twin_landed, twin, col).wait_recv()
    for side in range(2):
        units[1, side * half : (side + 1) * half, :] = full[1, side, 0:factors, :].T

    def mate_half(step, carry):
        place = other(z, LINE - 1 - step)
        partial[place] += image_block(1, place)

        @pl.when(step < LINE - 1)
        def _():
            remote(
                partial.at[place], arrived.at[z], image_sent.at[step], image_landed.at[z], row, line_col(place)
            ).start()

        return carry

    lax.fori_loop(0, LINE, mate_half, 0)

    image = partial[z]
    for step in range(1, LINE):
        place = other(z, step)
        remote(
            partial.at[place], arrived.at[place], image_sent.at[step], image_landed.at[place], row, line_col(place)
        ).wait_recv()
        image = image + arrived[place]

    loads[2].wait()
    local = lax.dot_general(
        image * weight_ref[...], image, (((1,), (1,)), ((), ())),
        precision=lax.Precision.HIGHEST, preferred_element_type=jnp.float32,
    )
    gram_line[z] = jnp.zeros(gram_line.shape[1:], jnp.float32)
    gram_line[z, :, 0:block] = local
    for step in range(1, LINE):
        there = line_col(other(z, step))
        send(remote(gram_line.at[z], gram_line.at[z], line_sent.at[step], line_landed.at[z], row, there))
    for step in range(1, LINE):
        place = other(z, step)
        remote(
            gram_line.at[place], gram_line.at[place], line_sent.at[step], line_landed.at[place], row, line_col(place)
        ).wait_recv()
    mine = row * 2 + y
    gram_group[mine] = (gram_line[0] + gram_line[1]) + (gram_line[2] + gram_line[3])
    for step in range(1, GROUP):
        there_row, there_y = other(row, step // 2), (y + step % 2) % 2
        send(
            remote(
                gram_group.at[mine], gram_group.at[mine], group_sent.at[step], group_landed.at[mine],
                there_row, z * 2 + there_y,
            )
        )
    for step in range(1, GROUP):
        there_row, there_y = other(row, step // 2), (y + step % 2) % 2
        slot = there_row * 2 + there_y
        remote(
            gram_group.at[slot], gram_group.at[slot], group_sent.at[step], group_landed.at[slot],
            there_row, z * 2 + there_y,
        ).wait_recv()
    gram = gram_group[0]
    for slot in range(1, GROUP):
        gram = gram + gram_group[slot]

    lanes = 128
    rank = lax.broadcasted_iota(jnp.int32, (block, lanes), 0)
    pivots = [jnp.broadcast_to(gram[:, k : k + 1], (block, lanes)) for k in range(block)]
    pieces = [image[:, left : left + lanes] for left in range(0, image.shape[1], lanes)]
    diagonal = jnp.ones((block, lanes), jnp.float32)
    for k in range(block):
        pivot = pivots[k][k : k + 1, :]
        diagonal = jnp.where(rank == k, pivot, diagonal)
        if k < block - 1:
            factor = jnp.where(rank > k, pivots[k] * (1.0 / pivot), 0.0)
            for later in range(k + 1, block):
                pivots[later] = pivots[later] - factor * pivots[later][k : k + 1, :]
            pieces = [piece - factor * piece[k : k + 1, :] for piece in pieces]
    root = lax.rsqrt(diagonal)
    for number, piece in enumerate(pieces):
        out_ref[:, number * lanes : (number + 1) * lanes] = piece * root

    for copy in sends:
        copy.wait_send()
    relay.wait_send()
    for step in range(LINE - 1):
        remote(partial.at[z], arrived.at[z], image_sent.at[step], image_landed.at[z], row, mate).wait_send()


def fused_per_device(strip_factors, sku_factors, probe, demand_weight):
    strip, factors = strip_factors.shape
    skus, part = sku_factors.shape
    columns = probe.shape[1]
    block = ROWS * columns
    bf16, f32 = jnp.bfloat16, jnp.float32
    dma = pltpu.SemaphoreType.DMA
    whole = pl.BlockSpec(memory_space=pltpu.VMEM)
    far = pl.BlockSpec(memory_space=pltpu.HBM)
    return pl.pallas_call(
        fused,
        out_shape=jax.ShapeDtypeStruct((block, strip), f32),
        in_specs=[far] * 4,
        out_specs=whole,
        scratch_shapes=[
            pltpu.VMEM((factors, strip), bf16),
            pltpu.VMEM((columns, skus), bf16),
            pltpu.VMEM((1, strip), f32),
            pltpu.VMEM((ROWS, part, skus), bf16),
            pltpu.VMEM((ROWS, block, skus // ROWS), bf16),
            pltpu.VMEM((block, skus // ROWS), f32),
            pltpu.VMEM((block, skus), f32),
            pltpu.VMEM((2, 2, factors + block, skus // 2), bf16),
            pltpu.VMEM((2, skus, factors), bf16),
            pltpu.VMEM((LINE, factors, strip), bf16),
            pltpu.VMEM((LINE, block, strip), f32),
            pltpu.VMEM((LINE, block, strip), f32),
            pltpu.VMEM((LINE, block, 128), f32),
            pltpu.VMEM((GROUP, block, 128), f32),
        ]
        + [dma((ROWS,))] * 4 + [dma((LINE,))] * 2 + [dma] * 4 + [dma((LINE,))] * 4 + [dma((GROUP,))] * 2 + [dma((4,))],
        compiler_params=pltpu.CompilerParams(
            collective_id=0, has_side_effects=True, vmem_limit_bytes=60 * 1024 * 1024
        ),
        cost_estimate=pl.CostEstimate(
            flops=2 * LINE * strip * 2 * skus * (factors + block),
            bytes_accessed=2 * (strip * factors + skus * part + skus * columns) + 4 * block * strip,
            transcendentals=LINE * strip * 2 * skus,
        ),
    )(strip_factors.T, sku_factors.T, probe.T, demand_weight)


def fits(mesh):
    return mesh.shape["row"] == ROWS and mesh.shape["col"] == 2 * LINE


def solution(mesh):
    placed = (P(("row", "col"), None), P("col", "row"), P("col", "row"), P(None, ("row", "col")))
    plan = fused_per_device if fits(mesh) else per_device
    return jax.shard_map(
        plan, mesh=mesh, in_specs=placed, out_specs=P(None, ("row", "col")), check_vma=False
    )
```

```python
import jax
import jax.numpy as jnp
from jax import lax
from jax.experimental import pallas as pl
from jax.experimental.pallas import tpu as pltpu
from jax.sharding import PartitionSpec as P

ROWS = 4
LINE = 4
GROUP = 2 * ROWS
CHUNK = 512


def unit_rows(factors):
    wide = factors.astype(jnp.float32)
    scale = lax.rsqrt(jnp.sum(wide * wide, axis=1, keepdims=True) + 1e-06)
    return (wide * scale).astype(jnp.bfloat16)


def per_device(strip_factors, sku_factors, probe, demand_weight):
    strip_unit = unit_rows(strip_factors)
    panel_raw, probe_cols = (
        lax.all_gather(sku_factors, "row", axis=1, tiled=True),
        lax.all_gather(probe, "row", axis=1, tiled=True),
    )
    sku_unit = unit_rows(panel_raw)
    columns = sku_unit.shape[0]
    width = min(512, columns)
    count = columns // width
    piece = lax.all_gather(strip_unit, "col", axis=0, tiled=True)
    total = jnp.zeros((probe_cols.shape[1], piece.shape[0]), jnp.float32)
    for number in range(count):
        panel = sku_unit[number * width : (number + 1) * width]
        block_probe = probe_cols[number * width : (number + 1) * width]
        corr = lax.dot_general(
            piece, panel, (((1,), (1,)), ((), ())), preferred_element_type=jnp.float32
        )
        affinity = jnp.exp(corr).astype(jnp.bfloat16)
        total = total + lax.dot_general(
            block_probe, affinity, (((0,), (1,)), ((), ())), preferred_element_type=jnp.float32
        )
    image = lax.psum_scatter(total, "col", scatter_dimension=1, tiled=True)
    local_gram = jnp.dot(image * demand_weight, image.T, precision=lax.Precision.HIGHEST)
    gram = lax.psum(local_gram, ("row", "col"))
    lower = jnp.linalg.cholesky(gram)
    return jax.scipy.linalg.solve_triangular(lower, image, lower=True)


def other(place, step):
    low = (place % 2 + step % 2) % 2
    high = (place // 2 + step // 2) % 2
    return 2 * high + low


def remote(source, target, sent, landed, row, col):
    return pltpu.make_async_remote_copy(
        src_ref=source,
        dst_ref=target,
        send_sem=sent,
        recv_sem=landed,
        device_id=(row, col),
        device_id_type=pl.DeviceIdType.MESH,
    )


def fused(
    strip_hbm, sku_ref, probe_hbm, weight_hbm, out_ref,
    strip_ref, probe_ref, weight_ref, raw, probe_raw, probe_stage, probe_wide, full, units, strips, partial, arrived, gram_line, gram_group,
    sku_sent, sku_landed, probe_sent, probe_landed, strip_sent, strip_landed,
    pair_sent, pair_landed, twin_sent, twin_landed, image_sent, image_landed,
    line_sent, line_landed, group_sent, group_landed, loaded,
):
    row, col = lax.axis_index("row"), lax.axis_index("col")
    core = row % 2
    z, y = col // 2, col % 2
    twin = row + 1 - 2 * core
    mate = col + 1 - 2 * y
    part, skus = sku_ref.shape
    columns = probe_ref.shape[0]
    loads = [
        pltpu.make_async_copy(source, target, loaded.at[number])
        for number, (source, target) in enumerate(
            ((strip_hbm, strip_ref), (probe_hbm, probe_ref), (weight_hbm, weight_ref), (sku_ref, raw.at[row]))
        )
    ]
    for load in loads:
        load.start()
    factors = ROWS * part
    block = ROWS * columns
    half = skus // 2
    fold = skus // ROWS

    def line_col(place):
        return place * 2 + y

    barrier = pltpu.get_barrier_semaphore()
    for step in range(1, ROWS):
        pl.semaphore_signal(barrier, inc=1, device_id=(other(row, step), col), device_id_type=pl.DeviceIdType.MESH)
    for step in range(1, LINE):
        pl.semaphore_signal(barrier, inc=1, device_id=(row, line_col(other(z, step))), device_id_type=pl.DeviceIdType.MESH)
    for step in range(ROWS):
        pl.semaphore_signal(barrier, inc=1, device_id=(other(row, step), mate), device_id_type=pl.DeviceIdType.MESH)

    loads[1].wait()
    for piece in range(ROWS):
        probe_stage[piece * columns : (piece + 1) * columns, :] = probe_ref[
            :, piece * fold : (piece + 1) * fold
        ].astype(jnp.float32)
    probe_raw[row] = probe_stage[...].astype(jnp.bfloat16)
    loads[0].wait()
    wide = strip_ref[...].astype(jnp.float32)
    scale = lax.rsqrt(jnp.sum(wide * wide, axis=0, keepdims=True) + 1e-06)
    strips[z] = (wide * scale).astype(jnp.bfloat16)

    pl.semaphore_wait(barrier, 2 * ROWS + LINE - 2)

    sends = []

    def send(copy):
        copy.start()
        sends.append(copy)

    def sku_copy(side, step, there, slot):
        lanes = slice(side * half, (side + 1) * half)
        return remote(
            sku_ref.at[:, lanes], raw.at[slot, :, lanes], sku_sent.at[side, step], sku_landed.at[side, slot], there, col
        )

    for step in (2, 3, 1):
        send(sku_copy(0, step, other(row, step), row))
    for step in (2, 3, 1):
        there = other(row, step)
        send(remote(probe_raw.at[row], probe_raw.at[row], probe_sent.at[step], probe_landed.at[row], there, col))
    for step in (2, 3, 1):
        send(sku_copy(1, step, other(row, step), row))
    for step in range(1, LINE):
        there = line_col(other(z, step))
        send(remote(strips.at[z], strips.at[z], strip_sent.at[step], strip_landed.at[z], row, there))

    loads[3].wait()
    for step in range(1, ROWS):
        there = other(row, step)
        remote(
            probe_raw.at[there], probe_raw.at[there], probe_sent.at[step], probe_landed.at[there], there, col
        ).wait_recv()
    for there in range(ROWS):
        folded = probe_raw[there].astype(jnp.float32)
        for piece in range(ROWS):
            probe_wide[there * columns : (there + 1) * columns, piece * fold : (piece + 1) * fold] = folded[
                piece * columns : (piece + 1) * columns
            ]

    pair = remote(full.at[0, core], full.at[1, core], pair_sent, pair_landed, row, mate)
    relay = remote(full.at[1, core], full.at[1, core], twin_sent, twin_landed, twin, col)

    def image_block(which, side, place):
        strip = strips[place]
        total = jnp.zeros((block, strip.shape[1]), jnp.float32)
        for first in range(0, half, CHUNK):
            corr = jnp.dot(units[which, side, first : first + CHUNK, :], strip, preferred_element_type=jnp.float32)
            affinity = jnp.exp(corr).astype(jnp.bfloat16)
            total = total + jnp.dot(
                full[which, side, factors:, first : first + CHUNK], affinity, preferred_element_type=jnp.float32
            )
        return total

    for side in range(2):
        for step in range(1, ROWS):
            there = other(row, step)
            sku_copy(side, step, there, there).wait_recv()
        lanes = slice(side * half, (side + 1) * half)
        wide = raw[:, :, lanes].reshape(factors, half).astype(jnp.float32)
        scale = lax.rsqrt(jnp.sum(wide * wide, axis=0, keepdims=True) + 1e-06)
        unit = (wide * scale).astype(jnp.bfloat16)
        full[0, side, 0:factors, :] = unit
        full[0, side, factors:, :] = probe_wide[:, lanes].astype(jnp.bfloat16)
        units[0, side] = unit.T

        @pl.when(core == side)
        def _():
            pair.start()

        def own_side(step, carry):
            place = other(z, step)
            if side == 0:

                @pl.when(step > 0)
                def _():
                    remote(
                        strips.at[place], strips.at[place], strip_sent.at[step], strip_landed.at[place],
                        row, line_col(place),
                    ).wait_recv()

                partial[place] = image_block(0, side, place)
            else:
                partial[place] += image_block(0, side, place)
            return carry

        lax.fori_loop(0, LINE, own_side, 0)

    pair.wait_recv()
    relay.start()
    units[1, core] = full[1, core, 0:factors, :].T

    def mate_first(step, carry):
        place = other(z, LINE - 1 - step)
        partial[place] += image_block(1, core, place)
        return carry

    lax.fori_loop(0, LINE, mate_first, 0)

    last = 1 - core
    remote(full.at[1, last], full.at[1, last], twin_sent, twin_landed, twin, col).wait_recv()
    units[1, last] = full[1, last, 0:factors, :].T

    def mate_last(step, carry):
        place = other(z, LINE - 1 - step)
        partial[place] += image_block(1, last, place)

        @pl.when(step < LINE - 1)
        def _():
            remote(
                partial.at[place], arrived.at[z], image_sent.at[step], image_landed.at[z], row, line_col(place)
            ).start()

        return carry

    lax.fori_loop(0, LINE, mate_last, 0)

    image = partial[z]
    for step in range(1, LINE):
        place = other(z, step)
        remote(
            partial.at[place], arrived.at[place], image_sent.at[step], image_landed.at[place], row, line_col(place)
        ).wait_recv()
        image = image + arrived[place]

    loads[2].wait()
    local = lax.dot_general(
        image * weight_ref[...], image, (((1,), (1,)), ((), ())),
        precision=lax.Precision.HIGHEST, preferred_element_type=jnp.float32,
    )
    gram_line[z] = jnp.zeros(gram_line.shape[1:], jnp.float32)
    gram_line[z, :, 0:block] = local
    for step in range(1, LINE):
        there = line_col(other(z, step))
        send(remote(gram_line.at[z], gram_line.at[z], line_sent.at[step], line_landed.at[z], row, there))
    for step in range(1, LINE):
        place = other(z, step)
        remote(
            gram_line.at[place], gram_line.at[place], line_sent.at[step], line_landed.at[place], row, line_col(place)
        ).wait_recv()
    mine = row * 2 + y
    gram_group[mine] = (gram_line[0] + gram_line[1]) + (gram_line[2] + gram_line[3])
    for step in range(1, GROUP):
        there_row, there_y = other(row, step // 2), (y + step % 2) % 2
        send(
            remote(
                gram_group.at[mine], gram_group.at[mine], group_sent.at[step], group_landed.at[mine],
                there_row, z * 2 + there_y,
            )
        )
    for step in range(1, GROUP):
        there_row, there_y = other(row, step // 2), (y + step % 2) % 2
        slot = there_row * 2 + there_y
        remote(
            gram_group.at[slot], gram_group.at[slot], group_sent.at[step], group_landed.at[slot],
            there_row, z * 2 + there_y,
        ).wait_recv()
    gram = gram_group[0]
    for slot in range(1, GROUP):
        gram = gram + gram_group[slot]

    lanes = 128
    rank = lax.broadcasted_iota(jnp.int32, (block, lanes), 0)
    pivots = [jnp.broadcast_to(gram[:, k : k + 1], (block, lanes)) for k in range(block)]
    pieces = [image[:, left : left + lanes] for left in range(0, image.shape[1], lanes)]
    diagonal = jnp.ones((block, lanes), jnp.float32)
    for k in range(block):
        pivot = pivots[k][k : k + 1, :]
        diagonal = jnp.where(rank == k, pivot, diagonal)
        if k < block - 1:
            factor = jnp.where(rank > k, pivots[k] * (1.0 / pivot), 0.0)
            for later in range(k + 1, block):
                pivots[later] = pivots[later] - factor * pivots[later][k : k + 1, :]
            pieces = [piece - factor * piece[k : k + 1, :] for piece in pieces]
    root = lax.rsqrt(diagonal)
    for number, piece in enumerate(pieces):
        out_ref[:, number * lanes : (number + 1) * lanes] = piece * root

    for copy in sends:
        copy.wait_send()
    pair.wait_send()
    relay.wait_send()
    for step in range(LINE - 1):
        remote(partial.at[z], arrived.at[z], image_sent.at[step], image_landed.at[z], row, mate).wait_send()


def fused_per_device(strip_factors, sku_factors, probe, demand_weight):
    strip, factors = strip_factors.shape
    skus, part = sku_factors.shape
    columns = probe.shape[1]
    block = ROWS * columns
    bf16, f32 = jnp.bfloat16, jnp.float32
    dma = pltpu.SemaphoreType.DMA
    whole = pl.BlockSpec(memory_space=pltpu.VMEM)
    far = pl.BlockSpec(memory_space=pltpu.HBM)
    return pl.pallas_call(
        fused,
        out_shape=pltpu.VMEM((block, strip), f32),
        in_specs=[far] * 4,
        out_specs=whole,
        scratch_shapes=[
            pltpu.VMEM((factors, strip), bf16),
            pltpu.VMEM((columns, skus), bf16),
            pltpu.VMEM((1, strip), f32),
            pltpu.VMEM((ROWS, part, skus), bf16),
            pltpu.VMEM((ROWS, block, skus // ROWS), bf16),
            pltpu.VMEM((block, skus // ROWS), f32),
            pltpu.VMEM((block, skus), f32),
            pltpu.VMEM((2, 2, factors + block, skus // 2), bf16),
            pltpu.VMEM((2, 2, skus // 2, factors), bf16),
            pltpu.VMEM((LINE, factors, strip), bf16),
            pltpu.VMEM((LINE, block, strip), f32),
            pltpu.VMEM((LINE, block, strip), f32),
            pltpu.VMEM((LINE, block, 128), f32),
            pltpu.VMEM((GROUP, block, 128), f32),
        ]
        + [dma((2, ROWS))] * 2 + [dma((ROWS,))] * 2 + [dma((LINE,))] * 2 + [dma] * 4 + [dma((LINE,))] * 4 + [dma((GROUP,))] * 2 + [dma((4,))],
        compiler_params=pltpu.CompilerParams(
            collective_id=0, has_side_effects=True, vmem_limit_bytes=60 * 1024 * 1024
        ),
        cost_estimate=pl.CostEstimate(
            flops=2 * LINE * strip * 2 * skus * (factors + block),
            bytes_accessed=2 * (strip * factors + skus * part + skus * columns) + 4 * block * strip,
            transcendentals=LINE * strip * 2 * skus,
        ),
    )(strip_factors.T, sku_factors.T, probe.T, demand_weight)


def fits(mesh):
    return mesh.shape["row"] == ROWS and mesh.shape["col"] == 2 * LINE


def solution(mesh):
    placed = (P(("row", "col"), None), P("col", "row"), P("col", "row"), P(None, ("row", "col")))
    plan = fused_per_device if fits(mesh) else per_device
    return jax.shard_map(
        plan, mesh=mesh, in_specs=placed, out_specs=P(None, ("row", "col")), check_vma=False
    )
```

```python
import jax
import jax.numpy as jnp
from jax import lax
from jax.experimental import pallas as pl
from jax.experimental.pallas import tpu as pltpu
from jax.sharding import PartitionSpec as P

ROWS = 4
LINE = 4
GROUP = 2 * ROWS
CHUNK = 1024
LOG2_E = 1.4426950408889634


def unit_rows(factors):
    wide = factors.astype(jnp.float32)
    scale = lax.rsqrt(jnp.sum(wide * wide, axis=1, keepdims=True) + 1e-06)
    return (wide * scale).astype(jnp.bfloat16)


def per_device(strip_factors, sku_factors, probe, demand_weight):
    strip_unit = unit_rows(strip_factors)
    panel_raw, probe_cols = (
        lax.all_gather(sku_factors, "row", axis=1, tiled=True),
        lax.all_gather(probe, "row", axis=1, tiled=True),
    )
    sku_unit = unit_rows(panel_raw)
    columns = sku_unit.shape[0]
    width = min(512, columns)
    count = columns // width
    piece = lax.all_gather(strip_unit, "col", axis=0, tiled=True)
    total = jnp.zeros((probe_cols.shape[1], piece.shape[0]), jnp.float32)
    for number in range(count):
        panel = sku_unit[number * width : (number + 1) * width]
        block_probe = probe_cols[number * width : (number + 1) * width]
        corr = lax.dot_general(
            piece, panel, (((1,), (1,)), ((), ())), preferred_element_type=jnp.float32
        )
        affinity = jnp.exp(corr).astype(jnp.bfloat16)
        total = total + lax.dot_general(
            block_probe, affinity, (((0,), (1,)), ((), ())), preferred_element_type=jnp.float32
        )
    image = lax.psum_scatter(total, "col", scatter_dimension=1, tiled=True)
    local_gram = jnp.dot(image * demand_weight, image.T, precision=lax.Precision.HIGHEST)
    gram = lax.psum(local_gram, ("row", "col"))
    lower = jnp.linalg.cholesky(gram)
    return jax.scipy.linalg.solve_triangular(lower, image, lower=True)


def other(place, step):
    low = (place % 2 + step % 2) % 2
    high = (place // 2 + step // 2) % 2
    return 2 * high + low


def remote(source, target, sent, landed, row, col):
    return pltpu.make_async_remote_copy(
        src_ref=source,
        dst_ref=target,
        send_sem=sent,
        recv_sem=landed,
        device_id=(row, col),
        device_id_type=pl.DeviceIdType.MESH,
    )


def fused(
    strip_hbm, sku_ref, probe_hbm, weight_hbm, out_ref,
    strip_ref, probe_ref, weight_ref, raw, probe_raw, probe_stage, probe_wide, full, units, strips, partial, arrived, gram_line, gram_group,
    sku_sent, sku_landed, probe_sent, probe_landed, strip_sent, strip_landed,
    pair_sent, pair_landed, twin_sent, twin_landed, image_sent, image_landed,
    line_sent, line_landed, group_sent, group_landed, loaded,
):
    row, col = lax.axis_index("row"), lax.axis_index("col")
    core = row % 2
    z, y = col // 2, col % 2
    twin = row + 1 - 2 * core
    mate = col + 1 - 2 * y
    part, skus = sku_ref.shape
    columns = probe_ref.shape[0]
    loads = [
        pltpu.make_async_copy(source, target, loaded.at[number])
        for number, (source, target) in enumerate(
            ((strip_hbm, strip_ref), (probe_hbm, probe_ref), (weight_hbm, weight_ref), (sku_ref, raw.at[row]))
        )
    ]
    for load in loads:
        load.start()
    factors = ROWS * part
    block = ROWS * columns
    half = skus // 2
    fold = skus // ROWS

    def line_col(place):
        return place * 2 + y

    barrier = pltpu.get_barrier_semaphore()
    for step in range(1, ROWS):
        pl.semaphore_signal(barrier, inc=1, device_id=(other(row, step), col), device_id_type=pl.DeviceIdType.MESH)
    for step in range(1, LINE):
        pl.semaphore_signal(barrier, inc=1, device_id=(row, line_col(other(z, step))), device_id_type=pl.DeviceIdType.MESH)
    for step in range(ROWS):
        pl.semaphore_signal(barrier, inc=1, device_id=(other(row, step), mate), device_id_type=pl.DeviceIdType.MESH)

    loads[1].wait()
    for piece in range(ROWS):
        probe_stage[piece * columns : (piece + 1) * columns, :] = probe_ref[
            :, piece * fold : (piece + 1) * fold
        ].astype(jnp.float32)
    probe_raw[row] = probe_stage[...].astype(jnp.bfloat16)
    loads[0].wait()
    wide = strip_ref[...].astype(jnp.float32)
    scale = lax.rsqrt(jnp.sum(wide * wide, axis=0, keepdims=True) + 1e-06)
    strips[z] = (wide * scale).astype(jnp.bfloat16)

    pl.semaphore_wait(barrier, 2 * ROWS + LINE - 2)

    sends = []

    def send(copy):
        copy.start()
        sends.append(copy)

    def sku_copy(side, step, there, slot):
        lanes = slice(side * half, (side + 1) * half)
        return remote(
            sku_ref.at[:, lanes], raw.at[slot, :, lanes], sku_sent.at[side, step], sku_landed.at[side, slot], there, col
        )

    for step in (2, 3, 1):
        send(sku_copy(0, step, other(row, step), row))
    for step in (2, 3, 1):
        there = other(row, step)
        send(remote(probe_raw.at[row], probe_raw.at[row], probe_sent.at[step], probe_landed.at[row], there, col))
    for step in (2, 3, 1):
        send(sku_copy(1, step, other(row, step), row))
    for step in range(1, LINE):
        there = line_col(other(z, step))
        send(remote(strips.at[z], strips.at[z], strip_sent.at[step], strip_landed.at[z], row, there))

    loads[3].wait()
    for step in range(1, ROWS):
        there = other(row, step)
        remote(
            probe_raw.at[there], probe_raw.at[there], probe_sent.at[step], probe_landed.at[there], there, col
        ).wait_recv()
    for there in range(ROWS):
        folded = probe_raw[there].astype(jnp.float32)
        for piece in range(ROWS):
            probe_wide[there * columns : (there + 1) * columns, piece * fold : (piece + 1) * fold] = folded[
                piece * columns : (piece + 1) * columns
            ]

    pair = remote(full.at[0, core], full.at[1, core], pair_sent, pair_landed, row, mate)
    relay = remote(full.at[1, core], full.at[1, core], twin_sent, twin_landed, twin, col)

    def image_block(which, side, place):
        strip = strips[place]
        total = jnp.zeros((block, strip.shape[1]), jnp.float32)
        for first in range(0, half, CHUNK):
            corr = jnp.dot(units[which, side, first : first + CHUNK, :], strip, preferred_element_type=jnp.float32)
            affinity = jnp.exp2(corr * LOG2_E).astype(jnp.bfloat16)
            total = total + jnp.dot(
                full[which, side, factors:, first : first + CHUNK], affinity, preferred_element_type=jnp.float32
            )
        return total

    for side in range(2):
        for step in range(1, ROWS):
            there = other(row, step)
            sku_copy(side, step, there, there).wait_recv()
        lanes = slice(side * half, (side + 1) * half)
        wide = raw[:, :, lanes].reshape(factors, half).astype(jnp.float32)
        scale = lax.rsqrt(jnp.sum(wide * wide, axis=0, keepdims=True) + 1e-06)
        unit = (wide * scale).astype(jnp.bfloat16)
        full[0, side, 0:factors, :] = unit
        full[0, side, factors:, :] = probe_wide[:, lanes].astype(jnp.bfloat16)
        units[0, side] = unit.T

        @pl.when(core == side)
        def _():
            pair.start()

        def own_side(step, carry):
            place = other(z, step)
            if side == 0:

                @pl.when(step > 0)
                def _():
                    remote(
                        strips.at[place], strips.at[place], strip_sent.at[step], strip_landed.at[place],
                        row, line_col(place),
                    ).wait_recv()

                partial[place] = image_block(0, side, place)
            else:
                partial[place] += image_block(0, side, place)
            return carry

        lax.fori_loop(0, LINE, own_side, 0)

    pair.wait_recv()
    relay.start()
    units[1, core] = full[1, core, 0:factors, :].T

    def mate_first(step, carry):
        place = other(z, LINE - 1 - step)
        partial[place] += image_block(1, core, place)
        return carry

    lax.fori_loop(0, LINE, mate_first, 0)

    last = 1 - core
    remote(full.at[1, last], full.at[1, last], twin_sent, twin_landed, twin, col).wait_recv()
    units[1, last] = full[1, last, 0:factors, :].T

    def mate_last(step, carry):
        place = other(z, LINE - 1 - step)
        partial[place] += image_block(1, last, place)

        @pl.when(step < LINE - 1)
        def _():
            remote(
                partial.at[place], arrived.at[z], image_sent.at[step], image_landed.at[z], row, line_col(place)
            ).start()

        return carry

    lax.fori_loop(0, LINE, mate_last, 0)

    image = partial[z]
    for step in range(1, LINE):
        place = other(z, step)
        remote(
            partial.at[place], arrived.at[place], image_sent.at[step], image_landed.at[place], row, line_col(place)
        ).wait_recv()
        image = image + arrived[place]

    loads[2].wait()
    local = lax.dot_general(
        image * weight_ref[...], image, (((1,), (1,)), ((), ())),
        precision=lax.Precision.HIGHEST, preferred_element_type=jnp.float32,
    )
    gram_line[z] = jnp.zeros(gram_line.shape[1:], jnp.float32)
    gram_line[z, :, 0:block] = local
    for step in range(1, LINE):
        there = line_col(other(z, step))
        send(remote(gram_line.at[z], gram_line.at[z], line_sent.at[step], line_landed.at[z], row, there))
    for step in range(1, LINE):
        place = other(z, step)
        remote(
            gram_line.at[place], gram_line.at[place], line_sent.at[step], line_landed.at[place], row, line_col(place)
        ).wait_recv()
    mine = row * 2 + y
    gram_group[mine] = (gram_line[0] + gram_line[1]) + (gram_line[2] + gram_line[3])
    for step in range(1, GROUP):
        there_row, there_y = other(row, step // 2), (y + step % 2) % 2
        send(
            remote(
                gram_group.at[mine], gram_group.at[mine], group_sent.at[step], group_landed.at[mine],
                there_row, z * 2 + there_y,
            )
        )
    for step in range(1, GROUP):
        there_row, there_y = other(row, step // 2), (y + step % 2) % 2
        slot = there_row * 2 + there_y
        remote(
            gram_group.at[slot], gram_group.at[slot], group_sent.at[step], group_landed.at[slot],
            there_row, z * 2 + there_y,
        ).wait_recv()
    gram = gram_group[0]
    for slot in range(1, GROUP):
        gram = gram + gram_group[slot]

    lanes = 128
    rank = lax.broadcasted_iota(jnp.int32, (block, lanes), 0)
    pivots = [jnp.broadcast_to(gram[:, k : k + 1], (block, lanes)) for k in range(block)]
    pieces = [image[:, left : left + lanes] for left in range(0, image.shape[1], lanes)]
    diagonal = jnp.ones((block, lanes), jnp.float32)
    for k in range(block):
        pivot = pivots[k][k : k + 1, :]
        diagonal = jnp.where(rank == k, pivot, diagonal)
        if k < block - 1:
            factor = jnp.where(rank > k, pivots[k] * (1.0 / pivot), 0.0)
            for later in range(k + 1, block):
                pivots[later] = pivots[later] - factor * pivots[later][k : k + 1, :]
            pieces = [piece - factor * piece[k : k + 1, :] for piece in pieces]
    root = lax.rsqrt(diagonal)
    for number, piece in enumerate(pieces):
        out_ref[:, number * lanes : (number + 1) * lanes] = piece * root

    for copy in sends:
        copy.wait_send()
    pair.wait_send()
    relay.wait_send()
    for step in range(LINE - 1):
        remote(partial.at[z], arrived.at[z], image_sent.at[step], image_landed.at[z], row, mate).wait_send()


def fused_per_device(strip_factors, sku_factors, probe, demand_weight):
    strip, factors = strip_factors.shape
    skus, part = sku_factors.shape
    columns = probe.shape[1]
    block = ROWS * columns
    bf16, f32 = jnp.bfloat16, jnp.float32
    dma = pltpu.SemaphoreType.DMA
    whole = pl.BlockSpec(memory_space=pltpu.VMEM)
    far = pl.BlockSpec(memory_space=pltpu.HBM)
    return pl.pallas_call(
        fused,
        out_shape=pltpu.VMEM((block, strip), f32),
        in_specs=[far] * 4,
        out_specs=whole,
        scratch_shapes=[
            pltpu.VMEM((factors, strip), bf16),
            pltpu.VMEM((columns, skus), bf16),
            pltpu.VMEM((1, strip), f32),
            pltpu.VMEM((ROWS, part, skus), bf16),
            pltpu.VMEM((ROWS, block, skus // ROWS), bf16),
            pltpu.VMEM((block, skus // ROWS), f32),
            pltpu.VMEM((block, skus), f32),
            pltpu.VMEM((2, 2, factors + block, skus // 2), bf16),
            pltpu.VMEM((2, 2, skus // 2, factors), bf16),
            pltpu.VMEM((LINE, factors, strip), bf16),
            pltpu.VMEM((LINE, block, strip), f32),
            pltpu.VMEM((LINE, block, strip), f32),
            pltpu.VMEM((LINE, block, 128), f32),
            pltpu.VMEM((GROUP, block, 128), f32),
        ]
        + [dma((2, ROWS))] * 2 + [dma((ROWS,))] * 2 + [dma((LINE,))] * 2 + [dma] * 4 + [dma((LINE,))] * 4 + [dma((GROUP,))] * 2 + [dma((4,))],
        compiler_params=pltpu.CompilerParams(
            collective_id=0, has_side_effects=True, vmem_limit_bytes=60 * 1024 * 1024
        ),
        cost_estimate=pl.CostEstimate(
            flops=2 * LINE * strip * 2 * skus * (factors + block),
            bytes_accessed=2 * (strip * factors + skus * part + skus * columns) + 4 * block * strip,
            transcendentals=LINE * strip * 2 * skus,
        ),
    )(strip_factors.T, sku_factors.T, probe.T, demand_weight)


def fits(mesh):
    return mesh.shape["row"] == ROWS and mesh.shape["col"] == 2 * LINE


def solution(mesh):
    placed = (P(("row", "col"), None), P("col", "row"), P("col", "row"), P(None, ("row", "col")))
    plan = fused_per_device if fits(mesh) else per_device
    return jax.shard_map(
        plan, mesh=mesh, in_specs=placed, out_specs=P(None, ("row", "col")), check_vma=False
    )
```

```python
import jax
import jax.numpy as jnp
from jax import lax
from jax.experimental import pallas as pl
from jax.experimental.pallas import tpu as pltpu
from jax.sharding import PartitionSpec as P

ROWS = 4
LINE = 4
GROUP = 2 * ROWS
LOG2_E = 1.4426950408889634


def unit_rows(factors):
    wide = factors.astype(jnp.float32)
    scale = lax.rsqrt(jnp.sum(wide * wide, axis=1, keepdims=True) + 1e-06)
    return (wide * scale).astype(jnp.bfloat16)


def per_device(strip_factors, sku_factors, probe, demand_weight):
    strip_unit = unit_rows(strip_factors)
    panel_raw, probe_cols = (
        lax.all_gather(sku_factors, "row", axis=1, tiled=True),
        lax.all_gather(probe, "row", axis=1, tiled=True),
    )
    sku_unit = unit_rows(panel_raw)
    columns = sku_unit.shape[0]
    width = min(512, columns)
    count = columns // width
    piece = lax.all_gather(strip_unit, "col", axis=0, tiled=True)
    total = jnp.zeros((probe_cols.shape[1], piece.shape[0]), jnp.float32)
    for number in range(count):
        panel = sku_unit[number * width : (number + 1) * width]
        block_probe = probe_cols[number * width : (number + 1) * width]
        corr = lax.dot_general(
            piece, panel, (((1,), (1,)), ((), ())), preferred_element_type=jnp.float32
        )
        affinity = jnp.exp(corr).astype(jnp.bfloat16)
        total = total + lax.dot_general(
            block_probe, affinity, (((0,), (1,)), ((), ())), preferred_element_type=jnp.float32
        )
    image = lax.psum_scatter(total, "col", scatter_dimension=1, tiled=True)
    local_gram = jnp.dot(image * demand_weight, image.T, precision=lax.Precision.HIGHEST)
    gram = lax.psum(local_gram, ("row", "col"))
    lower = jnp.linalg.cholesky(gram)
    return jax.scipy.linalg.solve_triangular(lower, image, lower=True)


def other(place, step):
    low = (place % 2 + step % 2) % 2
    high = (place // 2 + step // 2) % 2
    return 2 * high + low


def remote(source, target, sent, landed, row, col):
    return pltpu.make_async_remote_copy(
        src_ref=source,
        dst_ref=target,
        send_sem=sent,
        recv_sem=landed,
        device_id=(row, col),
        device_id_type=pl.DeviceIdType.MESH,
    )


def fused(
    strip_hbm, sku_ref, probe_hbm, weight_hbm, out_ref,
    strip_ref, probe_ref, weight_ref, raw, probe_raw, probe_stage, probe_wide, full, probes, strips, strips_tall, tall, partial, arrived, gram_line, gram_group,
    sku_sent, sku_landed, probe_sent, probe_landed, strip_sent, strip_landed,
    pair_sent, pair_landed, twin_sent, twin_landed, image_sent, image_landed,
    line_sent, line_landed, group_sent, group_landed, loaded,
):
    row, col = lax.axis_index("row"), lax.axis_index("col")
    core = row % 2
    z, y = col // 2, col % 2
    twin = row + 1 - 2 * core
    mate = col + 1 - 2 * y
    part, skus = sku_ref.shape
    columns = probe_ref.shape[0]
    loads = [
        pltpu.make_async_copy(source, target, loaded.at[number])
        for number, (source, target) in enumerate(
            ((strip_hbm, strip_ref), (probe_hbm, probe_ref), (weight_hbm, weight_ref), (sku_ref, raw.at[row]))
        )
    ]
    for load in loads:
        load.start()
    factors = ROWS * part
    block = ROWS * columns
    half = skus // 2
    fold = skus // ROWS

    def line_col(place):
        return place * 2 + y

    barrier = pltpu.get_barrier_semaphore()
    for step in range(1, ROWS):
        pl.semaphore_signal(barrier, inc=1, device_id=(other(row, step), col), device_id_type=pl.DeviceIdType.MESH)
    for step in range(1, LINE):
        pl.semaphore_signal(barrier, inc=1, device_id=(row, line_col(other(z, step))), device_id_type=pl.DeviceIdType.MESH)
    for step in range(ROWS):
        pl.semaphore_signal(barrier, inc=1, device_id=(other(row, step), mate), device_id_type=pl.DeviceIdType.MESH)

    loads[1].wait()
    for piece in range(ROWS):
        probe_stage[piece * columns : (piece + 1) * columns, :] = probe_ref[
            :, piece * fold : (piece + 1) * fold
        ].astype(jnp.float32)
    probe_raw[row] = probe_stage[...].astype(jnp.bfloat16)
    loads[0].wait()
    wide = strip_ref[...].astype(jnp.float32)
    scale = lax.rsqrt(jnp.sum(wide * wide, axis=0, keepdims=True) + 1e-06)
    strips[z] = (wide * scale).astype(jnp.bfloat16)

    pl.semaphore_wait(barrier, 2 * ROWS + LINE - 2)

    sends = []

    def send(copy):
        copy.start()
        sends.append(copy)

    def sku_copy(side, step, there, slot):
        lanes = slice(side * half, (side + 1) * half)
        return remote(
            sku_ref.at[:, lanes], raw.at[slot, :, lanes], sku_sent.at[side, step], sku_landed.at[side, slot], there, col
        )

    for step in (2, 3, 1):
        send(sku_copy(0, step, other(row, step), row))
    for step in (2, 3, 1):
        there = other(row, step)
        send(remote(probe_raw.at[row], probe_raw.at[row], probe_sent.at[step], probe_landed.at[row], there, col))
    for step in (2, 3, 1):
        send(sku_copy(1, step, other(row, step), row))
    for step in range(1, LINE):
        there = line_col(other(z, step))
        send(remote(strips.at[z], strips.at[z], strip_sent.at[step], strip_landed.at[z], row, there))

    loads[3].wait()
    for step in range(1, ROWS):
        there = other(row, step)
        remote(
            probe_raw.at[there], probe_raw.at[there], probe_sent.at[step], probe_landed.at[there], there, col
        ).wait_recv()
    for there in range(ROWS):
        folded = probe_raw[there].astype(jnp.float32)
        for piece in range(ROWS):
            probe_wide[there * columns : (there + 1) * columns, piece * fold : (piece + 1) * fold] = folded[
                piece * columns : (piece + 1) * columns
            ]

    pair = remote(full.at[0, core], full.at[1, core], pair_sent, pair_landed, row, mate)
    relay = remote(full.at[1, core], full.at[1, core], twin_sent, twin_landed, twin, col)

    def image_block(which, side, place):
        corr = jnp.dot(strips_tall[place], full[which, side, 0:factors, :], preferred_element_type=jnp.float32)
        affinity = jnp.exp2(corr * LOG2_E).astype(jnp.bfloat16)
        return jnp.dot(affinity, probes[which, side], preferred_element_type=jnp.float32)

    for side in range(2):
        for step in range(1, ROWS):
            there = other(row, step)
            sku_copy(side, step, there, there).wait_recv()
        lanes = slice(side * half, (side + 1) * half)
        wide = raw[:, :, lanes].reshape(factors, half).astype(jnp.float32)
        scale = lax.rsqrt(jnp.sum(wide * wide, axis=0, keepdims=True) + 1e-06)
        unit = (wide * scale).astype(jnp.bfloat16)
        full[0, side, 0:factors, :] = unit
        full[0, side, factors:, :] = probe_wide[:, lanes].astype(jnp.bfloat16)
        probes[0, side] = probe_wide[:, lanes].T.astype(jnp.bfloat16)

        @pl.when(core == side)
        def _():
            pair.start()

        def own_side(step, carry):
            place = other(z, step)
            if side == 0:

                @pl.when(step > 0)
                def _():
                    remote(
                        strips.at[place], strips.at[place], strip_sent.at[step], strip_landed.at[place],
                        row, line_col(place),
                    ).wait_recv()

                strips_tall[place] = strips[place].T
                tall[place] = image_block(0, side, place)
            else:
                tall[place] += image_block(0, side, place)
            return carry

        lax.fori_loop(0, LINE, own_side, 0)

    pair.wait_recv()
    relay.start()
    probes[1, core] = full[1, core, factors:, :].T

    def mate_first(step, carry):
        place = other(z, LINE - 1 - step)
        tall[place] += image_block(1, core, place)
        return carry

    lax.fori_loop(0, LINE, mate_first, 0)

    last = 1 - core
    remote(full.at[1, last], full.at[1, last], twin_sent, twin_landed, twin, col).wait_recv()
    probes[1, last] = full[1, last, factors:, :].T

    def mate_last(step, carry):
        place = other(z, LINE - 1 - step)
        partial[place] = (tall[place] + image_block(1, last, place)).T

        @pl.when(step < LINE - 1)
        def _():
            remote(
                partial.at[place], arrived.at[z], image_sent.at[step], image_landed.at[z], row, line_col(place)
            ).start()

        return carry

    lax.fori_loop(0, LINE, mate_last, 0)

    image = partial[z]
    for step in range(1, LINE):
        place = other(z, step)
        remote(
            partial.at[place], arrived.at[place], image_sent.at[step], image_landed.at[place], row, line_col(place)
        ).wait_recv()
        image = image + arrived[place]

    loads[2].wait()
    local = lax.dot_general(
        image * weight_ref[...], image, (((1,), (1,)), ((), ())),
        precision=lax.Precision.HIGHEST, preferred_element_type=jnp.float32,
    )
    gram_line[z] = jnp.zeros(gram_line.shape[1:], jnp.float32)
    gram_line[z, :, 0:block] = local
    for step in range(1, LINE):
        there = line_col(other(z, step))
        send(remote(gram_line.at[z], gram_line.at[z], line_sent.at[step], line_landed.at[z], row, there))
    for step in range(1, LINE):
        place = other(z, step)
        remote(
            gram_line.at[place], gram_line.at[place], line_sent.at[step], line_landed.at[place], row, line_col(place)
        ).wait_recv()
    mine = row * 2 + y
    gram_group[mine] = (gram_line[0] + gram_line[1]) + (gram_line[2] + gram_line[3])
    for step in range(1, GROUP):
        there_row, there_y = other(row, step // 2), (y + step % 2) % 2
        send(
            remote(
                gram_group.at[mine], gram_group.at[mine], group_sent.at[step], group_landed.at[mine],
                there_row, z * 2 + there_y,
            )
        )
    for step in range(1, GROUP):
        there_row, there_y = other(row, step // 2), (y + step % 2) % 2
        slot = there_row * 2 + there_y
        remote(
            gram_group.at[slot], gram_group.at[slot], group_sent.at[step], group_landed.at[slot],
            there_row, z * 2 + there_y,
        ).wait_recv()
    gram = gram_group[0]
    for slot in range(1, GROUP):
        gram = gram + gram_group[slot]

    lanes = 128
    rank = lax.broadcasted_iota(jnp.int32, (block, lanes), 0)
    pivots = [jnp.broadcast_to(gram[:, k : k + 1], (block, lanes)) for k in range(block)]
    pieces = [image[:, left : left + lanes] for left in range(0, image.shape[1], lanes)]
    diagonal = jnp.ones((block, lanes), jnp.float32)
    for k in range(block):
        pivot = pivots[k][k : k + 1, :]
        diagonal = jnp.where(rank == k, pivot, diagonal)
        if k < block - 1:
            factor = jnp.where(rank > k, pivots[k] * (1.0 / pivot), 0.0)
            for later in range(k + 1, block):
                pivots[later] = pivots[later] - factor * pivots[later][k : k + 1, :]
            pieces = [piece - factor * piece[k : k + 1, :] for piece in pieces]
    root = lax.rsqrt(diagonal)
    for number, piece in enumerate(pieces):
        out_ref[:, number * lanes : (number + 1) * lanes] = piece * root

    for copy in sends:
        copy.wait_send()
    pair.wait_send()
    relay.wait_send()
    for step in range(LINE - 1):
        remote(partial.at[z], arrived.at[z], image_sent.at[step], image_landed.at[z], row, mate).wait_send()


def fused_per_device(strip_factors, sku_factors, probe, demand_weight):
    strip, factors = strip_factors.shape
    skus, part = sku_factors.shape
    columns = probe.shape[1]
    block = ROWS * columns
    bf16, f32 = jnp.bfloat16, jnp.float32
    dma = pltpu.SemaphoreType.DMA
    whole = pl.BlockSpec(memory_space=pltpu.VMEM)
    far = pl.BlockSpec(memory_space=pltpu.HBM)
    return pl.pallas_call(
        fused,
        out_shape=pltpu.VMEM((block, strip), f32),
        in_specs=[far] * 4,
        out_specs=whole,
        scratch_shapes=[
            pltpu.VMEM((factors, strip), bf16),
            pltpu.VMEM((columns, skus), bf16),
            pltpu.VMEM((1, strip), f32),
            pltpu.VMEM((ROWS, part, skus), bf16),
            pltpu.VMEM((ROWS, block, skus // ROWS), bf16),
            pltpu.VMEM((block, skus // ROWS), f32),
            pltpu.VMEM((block, skus), f32),
            pltpu.VMEM((2, 2, factors + block, skus // 2), bf16),
            pltpu.VMEM((2, 2, skus // 2, block), bf16),
            pltpu.VMEM((LINE, factors, strip), bf16),
            pltpu.VMEM((LINE, strip, factors), bf16),
            pltpu.VMEM((LINE, strip, block), f32),
            pltpu.VMEM((LINE, block, strip), f32),
            pltpu.VMEM((LINE, block, strip), f32),
            pltpu.VMEM((LINE, block, 128), f32),
            pltpu.VMEM((GROUP, block, 128), f32),
        ]
        + [dma((2, ROWS))] * 2 + [dma((ROWS,))] * 2 + [dma((LINE,))] * 2 + [dma] * 4 + [dma((LINE,))] * 4 + [dma((GROUP,))] * 2 + [dma((4,))],
        compiler_params=pltpu.CompilerParams(
            collective_id=0, has_side_effects=True, vmem_limit_bytes=60 * 1024 * 1024
        ),
        cost_estimate=pl.CostEstimate(
            flops=2 * LINE * strip * 2 * skus * (factors + block),
            bytes_accessed=2 * (strip * factors + skus * part + skus * columns) + 4 * block * strip,
            transcendentals=LINE * strip * 2 * skus,
        ),
    )(strip_factors.T, sku_factors.T, probe.T, demand_weight)


def fits(mesh):
    return mesh.shape["row"] == ROWS and mesh.shape["col"] == 2 * LINE


def solution(mesh):
    placed = (P(("row", "col"), None), P("col", "row"), P("col", "row"), P(None, ("row", "col")))
    plan = fused_per_device if fits(mesh) else per_device
    return jax.shard_map(
        plan, mesh=mesh, in_specs=placed, out_specs=P(None, ("row", "col")), check_vma=False
    )
```

```python
import jax
import jax.numpy as jnp
from jax import lax
from jax.experimental import pallas as pl
from jax.experimental.pallas import tpu as pltpu
from jax.sharding import PartitionSpec as P

ROWS = 4
LINE = 4
GROUP = 2 * ROWS
CHUNK = 1024
LOG2_E = 1.4426950408889634


def unit_rows(factors):
    wide = factors.astype(jnp.float32)
    scale = lax.rsqrt(jnp.sum(wide * wide, axis=1, keepdims=True) + 1e-06)
    return (wide * scale).astype(jnp.bfloat16)


def per_device(strip_factors, sku_factors, probe, demand_weight):
    strip_unit = unit_rows(strip_factors)
    panel_raw, probe_cols = (
        lax.all_gather(sku_factors, "row", axis=1, tiled=True),
        lax.all_gather(probe, "row", axis=1, tiled=True),
    )
    sku_unit = unit_rows(panel_raw)
    columns = sku_unit.shape[0]
    width = min(512, columns)
    count = columns // width
    piece = lax.all_gather(strip_unit, "col", axis=0, tiled=True)
    total = jnp.zeros((probe_cols.shape[1], piece.shape[0]), jnp.float32)
    for number in range(count):
        panel = sku_unit[number * width : (number + 1) * width]
        block_probe = probe_cols[number * width : (number + 1) * width]
        corr = lax.dot_general(
            piece, panel, (((1,), (1,)), ((), ())), preferred_element_type=jnp.float32
        )
        affinity = jnp.exp(corr).astype(jnp.bfloat16)
        total = total + lax.dot_general(
            block_probe, affinity, (((0,), (1,)), ((), ())), preferred_element_type=jnp.float32
        )
    image = lax.psum_scatter(total, "col", scatter_dimension=1, tiled=True)
    local_gram = jnp.dot(image * demand_weight, image.T, precision=lax.Precision.HIGHEST)
    gram = lax.psum(local_gram, ("row", "col"))
    lower = jnp.linalg.cholesky(gram)
    return jax.scipy.linalg.solve_triangular(lower, image, lower=True)


def other(place, step):
    low = (place % 2 + step % 2) % 2
    high = (place // 2 + step // 2) % 2
    return 2 * high + low


def remote(source, target, sent, landed, row, col):
    return pltpu.make_async_remote_copy(
        src_ref=source,
        dst_ref=target,
        send_sem=sent,
        recv_sem=landed,
        device_id=(row, col),
        device_id_type=pl.DeviceIdType.MESH,
    )


def fused(
    strip_hbm, sku_ref, probe_hbm, weight_hbm, out_ref,
    strip_ref, probe_ref, weight_ref, raw, probe_raw, probe_stage, probe_wide, full, units, strips, partial, arrived, gram_line, gram_group,
    sku_sent, sku_landed, probe_sent, probe_landed, strip_sent, strip_landed,
    pair_sent, pair_landed, twin_sent, twin_landed, image_sent, image_landed,
    line_sent, line_landed, group_sent, group_landed, loaded,
):
    row, col = lax.axis_index("row"), lax.axis_index("col")
    core = row % 2
    z, y = col // 2, col % 2
    twin = row + 1 - 2 * core
    mate = col + 1 - 2 * y
    part, skus = sku_ref.shape
    columns = probe_ref.shape[0]
    loads = [
        pltpu.make_async_copy(source, target, loaded.at[number])
        for number, (source, target) in enumerate(
            ((strip_hbm, strip_ref), (probe_hbm, probe_ref), (weight_hbm, weight_ref), (sku_ref, raw.at[row]))
        )
    ]
    for load in loads:
        load.start()
    factors = ROWS * part
    block = ROWS * columns
    half = skus // 2
    fold = skus // ROWS

    def line_col(place):
        return place * 2 + y

    barrier = pltpu.get_barrier_semaphore()
    for step in range(1, ROWS):
        pl.semaphore_signal(barrier, inc=1, device_id=(other(row, step), col), device_id_type=pl.DeviceIdType.MESH)
    for step in range(1, LINE):
        pl.semaphore_signal(barrier, inc=1, device_id=(row, line_col(other(z, step))), device_id_type=pl.DeviceIdType.MESH)
    for step in range(ROWS):
        pl.semaphore_signal(barrier, inc=1, device_id=(other(row, step), mate), device_id_type=pl.DeviceIdType.MESH)

    sends = []

    def send(copy):
        copy.start()
        sends.append(copy)

    def sku_copy(side, step, there, slot):
        lanes = slice(side * half, (side + 1) * half)
        return remote(
            sku_ref.at[:, lanes], raw.at[slot, :, lanes], sku_sent.at[side, step], sku_landed.at[side, slot], there, col
        )

    pl.semaphore_wait(barrier, 2 * ROWS + LINE - 2)

    for step in (2, 3, 1):
        send(sku_copy(0, step, other(row, step), row))
    loads[1].wait()
    for piece in range(ROWS):
        probe_stage[piece * columns : (piece + 1) * columns, :] = probe_ref[
            :, piece * fold : (piece + 1) * fold
        ].astype(jnp.float32)
    probe_raw[row] = probe_stage[...].astype(jnp.bfloat16)
    for step in (2, 3, 1):
        there = other(row, step)
        send(remote(probe_raw.at[row], probe_raw.at[row], probe_sent.at[step], probe_landed.at[row], there, col))
    for step in (2, 3, 1):
        send(sku_copy(1, step, other(row, step), row))
    loads[0].wait()
    wide = strip_ref[...].astype(jnp.float32)
    scale = lax.rsqrt(jnp.sum(wide * wide, axis=0, keepdims=True) + 1e-06)
    strips[z] = (wide * scale).astype(jnp.bfloat16)
    for step in range(1, LINE):
        there = line_col(other(z, step))
        send(remote(strips.at[z], strips.at[z], strip_sent.at[step], strip_landed.at[z], row, there))

    loads[3].wait()
    for step in range(1, ROWS):
        there = other(row, step)
        remote(
            probe_raw.at[there], probe_raw.at[there], probe_sent.at[step], probe_landed.at[there], there, col
        ).wait_recv()
    for there in range(ROWS):
        folded = probe_raw[there].astype(jnp.float32)
        for piece in range(ROWS):
            probe_wide[there * columns : (there + 1) * columns, piece * fold : (piece + 1) * fold] = folded[
                piece * columns : (piece + 1) * columns
            ]

    pair = remote(full.at[0, core], full.at[1, core], pair_sent, pair_landed, row, mate)
    relay = remote(full.at[1, core], full.at[1, core], twin_sent, twin_landed, twin, col)

    def image_block(which, side, place):
        strip = strips[place]
        total = jnp.zeros((block, strip.shape[1]), jnp.float32)
        for first in range(0, half, CHUNK):
            corr = jnp.dot(units[which, side, first : first + CHUNK, :], strip, preferred_element_type=jnp.float32)
            affinity = jnp.exp2(corr * LOG2_E).astype(jnp.bfloat16)
            total = total + jnp.dot(
                full[which, side, factors:, first : first + CHUNK], affinity, preferred_element_type=jnp.float32
            )
        return total

    for side in range(2):
        for step in range(1, ROWS):
            there = other(row, step)
            sku_copy(side, step, there, there).wait_recv()
        lanes = slice(side * half, (side + 1) * half)
        wide = raw[:, :, lanes].reshape(factors, half).astype(jnp.float32)
        scale = lax.rsqrt(jnp.sum(wide * wide, axis=0, keepdims=True) + 1e-06)
        unit = (wide * scale).astype(jnp.bfloat16)
        full[0, side, 0:factors, :] = unit
        full[0, side, factors:, :] = probe_wide[:, lanes].astype(jnp.bfloat16)
        units[0, side] = unit.T

        @pl.when(core == side)
        def _():
            pair.start()

        def own_side(step, carry):
            place = other(z, step)
            if side == 0:

                @pl.when(step > 0)
                def _():
                    remote(
                        strips.at[place], strips.at[place], strip_sent.at[step], strip_landed.at[place],
                        row, line_col(place),
                    ).wait_recv()

                partial[place] = image_block(0, side, place)
            else:
                partial[place] += image_block(0, side, place)
            return carry

        lax.fori_loop(side, LINE, own_side, 0)

    pair.wait_recv()
    relay.start()
    units[1, core] = full[1, core, 0:factors, :].T

    def mate_first(step, carry):
        place = other(z, LINE - 1 - step)
        partial[place] += image_block(1, core, place)
        return carry

    lax.fori_loop(0, LINE - 1, mate_first, 0)

    last = 1 - core
    remote(full.at[1, last], full.at[1, last], twin_sent, twin_landed, twin, col).wait_recv()
    units[1, last] = full[1, last, 0:factors, :].T

    def mate_last(step, carry):
        place = other(z, LINE - 1 - step)
        partial[place] += image_block(1, last, place)

        remote(
            partial.at[place], arrived.at[z], image_sent.at[step], image_landed.at[z], row, line_col(place)
        ).start()
        return carry

    lax.fori_loop(0, LINE - 1, mate_last, 0)

    image = partial[z] + image_block(0, 1, z) + image_block(1, 0, z) + image_block(1, 1, z)
    for step in range(1, LINE):
        place = other(z, step)
        remote(
            partial.at[place], arrived.at[place], image_sent.at[step], image_landed.at[place], row, line_col(place)
        ).wait_recv()
        image = image + arrived[place]

    loads[2].wait()
    local = lax.dot_general(
        image * weight_ref[...], image, (((1,), (1,)), ((), ())),
        precision=lax.Precision.HIGHEST, preferred_element_type=jnp.float32,
    )
    gram_line[z] = jnp.zeros(gram_line.shape[1:], jnp.float32)
    gram_line[z, :, 0:block] = local
    for step in range(1, LINE):
        there = line_col(other(z, step))
        send(remote(gram_line.at[z], gram_line.at[z], line_sent.at[step], line_landed.at[z], row, there))
    for step in range(1, LINE):
        place = other(z, step)
        remote(
            gram_line.at[place], gram_line.at[place], line_sent.at[step], line_landed.at[place], row, line_col(place)
        ).wait_recv()
    mine = row * 2 + y
    gram_group[mine] = (gram_line[0] + gram_line[1]) + (gram_line[2] + gram_line[3])
    for step in range(1, GROUP):
        there_row, there_y = other(row, step // 2), (y + step % 2) % 2
        send(
            remote(
                gram_group.at[mine], gram_group.at[mine], group_sent.at[step], group_landed.at[mine],
                there_row, z * 2 + there_y,
            )
        )
    for step in range(1, GROUP):
        there_row, there_y = other(row, step // 2), (y + step % 2) % 2
        slot = there_row * 2 + there_y
        remote(
            gram_group.at[slot], gram_group.at[slot], group_sent.at[step], group_landed.at[slot],
            there_row, z * 2 + there_y,
        ).wait_recv()
    gram = gram_group[0]
    for slot in range(1, GROUP):
        gram = gram + gram_group[slot]

    lanes = 128
    rank = lax.broadcasted_iota(jnp.int32, (block, lanes), 0)
    pivots = [jnp.broadcast_to(gram[:, k : k + 1], (block, lanes)) for k in range(block)]
    pieces = [image[:, left : left + lanes] for left in range(0, image.shape[1], lanes)]
    diagonal = jnp.ones((block, lanes), jnp.float32)
    for k in range(block):
        pivot = pivots[k][k : k + 1, :]
        diagonal = jnp.where(rank == k, pivot, diagonal)
        if k < block - 1:
            factor = jnp.where(rank > k, pivots[k] * (1.0 / pivot), 0.0)
            for later in range(k + 1, block):
                pivots[later] = pivots[later] - factor * pivots[later][k : k + 1, :]
            pieces = [piece - factor * piece[k : k + 1, :] for piece in pieces]
    root = lax.rsqrt(diagonal)
    for number, piece in enumerate(pieces):
        out_ref[:, number * lanes : (number + 1) * lanes] = piece * root

    for copy in sends:
        copy.wait_send()
    pair.wait_send()
    relay.wait_send()
    for step in range(LINE - 1):
        remote(partial.at[z], arrived.at[z], image_sent.at[step], image_landed.at[z], row, mate).wait_send()


def fused_per_device(strip_factors, sku_factors, probe, demand_weight):
    strip, factors = strip_factors.shape
    skus, part = sku_factors.shape
    columns = probe.shape[1]
    block = ROWS * columns
    bf16, f32 = jnp.bfloat16, jnp.float32
    dma = pltpu.SemaphoreType.DMA
    whole = pl.BlockSpec(memory_space=pltpu.VMEM)
    far = pl.BlockSpec(memory_space=pltpu.HBM)
    return pl.pallas_call(
        fused,
        out_shape=pltpu.VMEM((block, strip), f32),
        in_specs=[far] * 4,
        out_specs=whole,
        scratch_shapes=[
            pltpu.VMEM((factors, strip), bf16),
            pltpu.VMEM((columns, skus), bf16),
            pltpu.VMEM((1, strip), f32),
            pltpu.VMEM((ROWS, part, skus), bf16),
            pltpu.VMEM((ROWS, block, skus // ROWS), bf16),
            pltpu.VMEM((block, skus // ROWS), f32),
            pltpu.VMEM((block, skus), f32),
            pltpu.VMEM((2, 2, factors + block, skus // 2), bf16),
            pltpu.VMEM((2, 2, skus // 2, factors), bf16),
            pltpu.VMEM((LINE, factors, strip), bf16),
            pltpu.VMEM((LINE, block, strip), f32),
            pltpu.VMEM((LINE, block, strip), f32),
            pltpu.VMEM((LINE, block, 128), f32),
            pltpu.VMEM((GROUP, block, 128), f32),
        ]
        + [dma((2, ROWS))] * 2 + [dma((ROWS,))] * 2 + [dma((LINE,))] * 2 + [dma] * 4 + [dma((LINE,))] * 4 + [dma((GROUP,))] * 2 + [dma((4,))],
        compiler_params=pltpu.CompilerParams(
            collective_id=0, has_side_effects=True, vmem_limit_bytes=60 * 1024 * 1024
        ),
        cost_estimate=pl.CostEstimate(
            flops=2 * LINE * strip * 2 * skus * (factors + block),
            bytes_accessed=2 * (strip * factors + skus * part + skus * columns) + 4 * block * strip,
            transcendentals=LINE * strip * 2 * skus,
        ),
    )(strip_factors.T, sku_factors.T, probe.T, demand_weight)


def fits(mesh):
    return mesh.shape["row"] == ROWS and mesh.shape["col"] == 2 * LINE


def solution(mesh):
    placed = (P(("row", "col"), None), P("col", "row"), P("col", "row"), P(None, ("row", "col")))
    plan = fused_per_device if fits(mesh) else per_device
    return jax.shard_map(
        plan, mesh=mesh, in_specs=placed, out_specs=P(None, ("row", "col")), check_vma=False
    )
```

```python
import jax
import jax.numpy as jnp
from jax import lax
from jax.experimental import pallas as pl
from jax.experimental.pallas import tpu as pltpu
from jax.sharding import PartitionSpec as P

ROWS = 4
LINE = 4
GROUP = 2 * ROWS
CHUNK = 256
LOG2_E = 1.4426950408889634


def unit_rows(factors):
    wide = factors.astype(jnp.float32)
    scale = lax.rsqrt(jnp.sum(wide * wide, axis=1, keepdims=True) + 1e-06)
    return (wide * scale).astype(jnp.bfloat16)


def per_device(strip_factors, sku_factors, probe, demand_weight):
    strip_unit = unit_rows(strip_factors)
    panel_raw, probe_cols = (
        lax.all_gather(sku_factors, "row", axis=1, tiled=True),
        lax.all_gather(probe, "row", axis=1, tiled=True),
    )
    sku_unit = unit_rows(panel_raw)
    columns = sku_unit.shape[0]
    width = min(512, columns)
    count = columns // width
    piece = lax.all_gather(strip_unit, "col", axis=0, tiled=True)
    total = jnp.zeros((probe_cols.shape[1], piece.shape[0]), jnp.float32)
    for number in range(count):
        panel = sku_unit[number * width : (number + 1) * width]
        block_probe = probe_cols[number * width : (number + 1) * width]
        corr = lax.dot_general(
            piece, panel, (((1,), (1,)), ((), ())), preferred_element_type=jnp.float32
        )
        affinity = jnp.exp(corr).astype(jnp.bfloat16)
        total = total + lax.dot_general(
            block_probe, affinity, (((0,), (1,)), ((), ())), preferred_element_type=jnp.float32
        )
    image = lax.psum_scatter(total, "col", scatter_dimension=1, tiled=True)
    local_gram = jnp.dot(image * demand_weight, image.T, precision=lax.Precision.HIGHEST)
    gram = lax.psum(local_gram, ("row", "col"))
    lower = jnp.linalg.cholesky(gram)
    return jax.scipy.linalg.solve_triangular(lower, image, lower=True)


def other(place, step):
    low = (place % 2 + step % 2) % 2
    high = (place // 2 + step // 2) % 2
    return 2 * high + low


def remote(source, target, sent, landed, row, col):
    return pltpu.make_async_remote_copy(
        src_ref=source,
        dst_ref=target,
        send_sem=sent,
        recv_sem=landed,
        device_id=(row, col),
        device_id_type=pl.DeviceIdType.MESH,
    )


def fused(
    strip_hbm, sku_ref, probe_hbm, weight_hbm, out_ref,
    strip_ref, probe_ref, weight_ref, raw, probe_raw, probe_stage, probe_wide, full, units, strips, partial, arrived, gram_line, gram_group,
    sku_sent, sku_landed, probe_sent, probe_landed, strip_sent, strip_landed,
    pair_sent, pair_landed, twin_sent, twin_landed, image_sent, image_landed,
    line_sent, line_landed, group_sent, group_landed, loaded,
):
    row, col = lax.axis_index("row"), lax.axis_index("col")
    core = row % 2
    z, y = col // 2, col % 2
    twin = row + 1 - 2 * core
    mate = col + 1 - 2 * y
    part, skus = sku_ref.shape
    columns = probe_ref.shape[0]
    loads = [
        pltpu.make_async_copy(source, target, loaded.at[number])
        for number, (source, target) in enumerate(
            ((strip_hbm, strip_ref), (probe_hbm, probe_ref), (weight_hbm, weight_ref), (sku_ref, raw.at[row]))
        )
    ]
    for load in loads:
        load.start()
    factors = ROWS * part
    block = ROWS * columns
    half = skus // 2
    fold = skus // ROWS

    def line_col(place):
        return place * 2 + y

    barrier = pltpu.get_barrier_semaphore()
    for step in range(1, ROWS):
        pl.semaphore_signal(barrier, inc=1, device_id=(other(row, step), col), device_id_type=pl.DeviceIdType.MESH)
    for step in range(1, LINE):
        pl.semaphore_signal(barrier, inc=1, device_id=(row, line_col(other(z, step))), device_id_type=pl.DeviceIdType.MESH)
    for step in range(ROWS):
        pl.semaphore_signal(barrier, inc=1, device_id=(other(row, step), mate), device_id_type=pl.DeviceIdType.MESH)

    sends = []

    def send(copy):
        copy.start()
        sends.append(copy)

    def sku_copy(side, step, there, slot):
        lanes = slice(side * half, (side + 1) * half)
        return remote(
            sku_ref.at[:, lanes], raw.at[slot, :, lanes], sku_sent.at[side, step], sku_landed.at[side, slot], there, col
        )

    pl.semaphore_wait(barrier, 2 * ROWS + LINE - 2)

    for step in (2, 3, 1):
        send(sku_copy(0, step, other(row, step), row))
    loads[1].wait()
    for piece in range(ROWS):
        probe_stage[piece * columns : (piece + 1) * columns, :] = probe_ref[
            :, piece * fold : (piece + 1) * fold
        ].astype(jnp.float32)
    probe_raw[row] = probe_stage[...].astype(jnp.bfloat16)
    for step in (2, 3, 1):
        there = other(row, step)
        send(remote(probe_raw.at[row], probe_raw.at[row], probe_sent.at[step], probe_landed.at[row], there, col))
    for step in (2, 3, 1):
        send(sku_copy(1, step, other(row, step), row))
    loads[0].wait()
    wide = strip_ref[...].astype(jnp.float32)
    scale = lax.rsqrt(jnp.sum(wide * wide, axis=0, keepdims=True) + 1e-06)
    strips[z] = (wide * scale).astype(jnp.bfloat16)
    for step in range(1, LINE):
        there = line_col(other(z, step))
        send(remote(strips.at[z], strips.at[z], strip_sent.at[step], strip_landed.at[z], row, there))

    loads[3].wait()
    for step in range(1, ROWS):
        there = other(row, step)
        remote(
            probe_raw.at[there], probe_raw.at[there], probe_sent.at[step], probe_landed.at[there], there, col
        ).wait_recv()
    for there in range(ROWS):
        folded = probe_raw[there].astype(jnp.float32)
        for piece in range(ROWS):
            probe_wide[there * columns : (there + 1) * columns, piece * fold : (piece + 1) * fold] = folded[
                piece * columns : (piece + 1) * columns
            ]

    pair = remote(full.at[0, core], full.at[1, core], pair_sent, pair_landed, row, mate)
    relay = remote(full.at[1, core], full.at[1, core], twin_sent, twin_landed, twin, col)

    def image_blocks(tasks):
        steps = [(number, first) for number in range(len(tasks)) for first in range(0, half, CHUNK)]
        totals = [jnp.zeros((block, strips.shape[2]), jnp.float32) for _ in tasks]
        corr = affinity = None
        for turn in range(len(steps) + 2):
            corr_next = affinity_next = None
            if turn < len(steps):
                number, first = steps[turn]
                which, side, place = tasks[number]
                corr_next = jnp.dot(
                    units[which, side, first : first + CHUNK, :], strips[place], preferred_element_type=jnp.float32
                )
            if corr is not None:
                affinity_next = jnp.exp2(corr * LOG2_E).astype(jnp.bfloat16)
            if affinity is not None:
                number, first = steps[turn - 2]
                which, side, place = tasks[number]
                totals[number] = totals[number] + jnp.dot(
                    full[which, side, factors:, first : first + CHUNK], affinity, preferred_element_type=jnp.float32
                )
            corr, affinity = corr_next, affinity_next
        return totals

    def image_block(which, side, place):
        return image_blocks([(which, side, place)])[0]

    for side in range(2):
        for step in range(1, ROWS):
            there = other(row, step)
            sku_copy(side, step, there, there).wait_recv()
        lanes = slice(side * half, (side + 1) * half)
        wide = raw[:, :, lanes].reshape(factors, half).astype(jnp.float32)
        scale = lax.rsqrt(jnp.sum(wide * wide, axis=0, keepdims=True) + 1e-06)
        unit = (wide * scale).astype(jnp.bfloat16)
        full[0, side, 0:factors, :] = unit
        full[0, side, factors:, :] = probe_wide[:, lanes].astype(jnp.bfloat16)
        units[0, side] = unit.T

        @pl.when(core == side)
        def _():
            pair.start()

        if side == 0:

            def own_side(step, carry):
                place = other(z, step)

                @pl.when(step > 0)
                def _():
                    remote(
                        strips.at[place], strips.at[place], strip_sent.at[step], strip_landed.at[place],
                        row, line_col(place),
                    ).wait_recv()

                partial[place] = image_block(0, side, place)
                return carry

            lax.fori_loop(0, LINE, own_side, 0)
        else:
            places = [other(z, step) for step in range(1, LINE)]
            for place, total in zip(places, image_blocks([(0, side, place) for place in places])):
                partial[place] += total

    pair.wait_recv()
    relay.start()
    units[1, core] = full[1, core, 0:factors, :].T

    for place, total in zip(places, image_blocks([(1, core, place) for place in places])):
        partial[place] += total

    last = 1 - core
    remote(full.at[1, last], full.at[1, last], twin_sent, twin_landed, twin, col).wait_recv()
    units[1, last] = full[1, last, 0:factors, :].T

    def mate_last(step, carry):
        place = other(z, LINE - 1 - step)
        partial[place] += image_block(1, last, place)

        remote(
            partial.at[place], arrived.at[z], image_sent.at[step], image_landed.at[z], row, line_col(place)
        ).start()
        return carry

    lax.fori_loop(0, LINE - 1, mate_last, 0)

    image = partial[z] + sum(image_blocks([(0, 1, z), (1, 0, z), (1, 1, z)]))
    for step in range(1, LINE):
        place = other(z, step)
        remote(
            partial.at[place], arrived.at[place], image_sent.at[step], image_landed.at[place], row, line_col(place)
        ).wait_recv()
        image = image + arrived[place]

    loads[2].wait()
    local = lax.dot_general(
        image * weight_ref[...], image, (((1,), (1,)), ((), ())),
        precision=lax.Precision.HIGHEST, preferred_element_type=jnp.float32,
    )
    gram_line[z] = jnp.zeros(gram_line.shape[1:], jnp.float32)
    gram_line[z, :, 0:block] = local
    for step in range(1, LINE):
        there = line_col(other(z, step))
        send(remote(gram_line.at[z], gram_line.at[z], line_sent.at[step], line_landed.at[z], row, there))
    for step in range(1, LINE):
        place = other(z, step)
        remote(
            gram_line.at[place], gram_line.at[place], line_sent.at[step], line_landed.at[place], row, line_col(place)
        ).wait_recv()
    mine = row * 2 + y
    gram_group[mine] = (gram_line[0] + gram_line[1]) + (gram_line[2] + gram_line[3])
    for step in range(1, GROUP):
        there_row, there_y = other(row, step // 2), (y + step % 2) % 2
        send(
            remote(
                gram_group.at[mine], gram_group.at[mine], group_sent.at[step], group_landed.at[mine],
                there_row, z * 2 + there_y,
            )
        )
    for step in range(1, GROUP):
        there_row, there_y = other(row, step // 2), (y + step % 2) % 2
        slot = there_row * 2 + there_y
        remote(
            gram_group.at[slot], gram_group.at[slot], group_sent.at[step], group_landed.at[slot],
            there_row, z * 2 + there_y,
        ).wait_recv()
    gram = gram_group[0]
    for slot in range(1, GROUP):
        gram = gram + gram_group[slot]

    lanes = 128
    rank = lax.broadcasted_iota(jnp.int32, (block, lanes), 0)
    pivots = [jnp.broadcast_to(gram[:, k : k + 1], (block, lanes)) for k in range(block)]
    pieces = [image[:, left : left + lanes] for left in range(0, image.shape[1], lanes)]
    diagonal = jnp.ones((block, lanes), jnp.float32)
    for k in range(block):
        pivot = pivots[k][k : k + 1, :]
        diagonal = jnp.where(rank == k, pivot, diagonal)
        if k < block - 1:
            factor = jnp.where(rank > k, pivots[k] * (1.0 / pivot), 0.0)
            for later in range(k + 1, block):
                pivots[later] = pivots[later] - factor * pivots[later][k : k + 1, :]
            pieces = [piece - factor * piece[k : k + 1, :] for piece in pieces]
    root = lax.rsqrt(diagonal)
    for number, piece in enumerate(pieces):
        out_ref[:, number * lanes : (number + 1) * lanes] = piece * root

    for copy in sends:
        copy.wait_send()
    pair.wait_send()
    relay.wait_send()
    for step in range(LINE - 1):
        remote(partial.at[z], arrived.at[z], image_sent.at[step], image_landed.at[z], row, mate).wait_send()


def fused_per_device(strip_factors, sku_factors, probe, demand_weight):
    strip, factors = strip_factors.shape
    skus, part = sku_factors.shape
    columns = probe.shape[1]
    block = ROWS * columns
    bf16, f32 = jnp.bfloat16, jnp.float32
    dma = pltpu.SemaphoreType.DMA
    whole = pl.BlockSpec(memory_space=pltpu.VMEM)
    far = pl.BlockSpec(memory_space=pltpu.HBM)
    return pl.pallas_call(
        fused,
        out_shape=pltpu.VMEM((block, strip), f32),
        in_specs=[far] * 4,
        out_specs=whole,
        scratch_shapes=[
            pltpu.VMEM((factors, strip), bf16),
            pltpu.VMEM((columns, skus), bf16),
            pltpu.VMEM((1, strip), f32),
            pltpu.VMEM((ROWS, part, skus), bf16),
            pltpu.VMEM((ROWS, block, skus // ROWS), bf16),
            pltpu.VMEM((block, skus // ROWS), f32),
            pltpu.VMEM((block, skus), f32),
            pltpu.VMEM((2, 2, factors + block, skus // 2), bf16),
            pltpu.VMEM((2, 2, skus // 2, factors), bf16),
            pltpu.VMEM((LINE, factors, strip), bf16),
            pltpu.VMEM((LINE, block, strip), f32),
            pltpu.VMEM((LINE, block, strip), f32),
            pltpu.VMEM((LINE, block, 128), f32),
            pltpu.VMEM((GROUP, block, 128), f32),
        ]
        + [dma((2, ROWS))] * 2 + [dma((ROWS,))] * 2 + [dma((LINE,))] * 2 + [dma] * 4 + [dma((LINE,))] * 4 + [dma((GROUP,))] * 2 + [dma((4,))],
        compiler_params=pltpu.CompilerParams(
            collective_id=0, has_side_effects=True, vmem_limit_bytes=60 * 1024 * 1024
        ),
        cost_estimate=pl.CostEstimate(
            flops=2 * LINE * strip * 2 * skus * (factors + block),
            bytes_accessed=2 * (strip * factors + skus * part + skus * columns) + 4 * block * strip,
            transcendentals=LINE * strip * 2 * skus,
        ),
    )(strip_factors.T, sku_factors.T, probe.T, demand_weight)


def fits(mesh):
    return mesh.shape["row"] == ROWS and mesh.shape["col"] == 2 * LINE


def solution(mesh):
    placed = (P(("row", "col"), None), P("col", "row"), P("col", "row"), P(None, ("row", "col")))
    plan = fused_per_device if fits(mesh) else per_device
    return jax.shard_map(
        plan, mesh=mesh, in_specs=placed, out_specs=P(None, ("row", "col")), check_vma=False
    )
```

```python
import jax
import jax.numpy as jnp
from jax import lax
from jax.experimental import pallas as pl
from jax.experimental.pallas import tpu as pltpu
from jax.sharding import PartitionSpec as P

ROWS = 4
LINE = 4
GROUP = 2 * ROWS
CHUNK = 256
LOG2_E = 1.4426950408889634


def unit_rows(factors):
    wide = factors.astype(jnp.float32)
    scale = lax.rsqrt(jnp.sum(wide * wide, axis=1, keepdims=True) + 1e-06)
    return (wide * scale).astype(jnp.bfloat16)


def per_device(strip_factors, sku_factors, probe, demand_weight):
    strip_unit = unit_rows(strip_factors)
    panel_raw, probe_cols = (
        lax.all_gather(sku_factors, "row", axis=1, tiled=True),
        lax.all_gather(probe, "row", axis=1, tiled=True),
    )
    sku_unit = unit_rows(panel_raw)
    columns = sku_unit.shape[0]
    width = min(512, columns)
    count = columns // width
    piece = lax.all_gather(strip_unit, "col", axis=0, tiled=True)
    total = jnp.zeros((probe_cols.shape[1], piece.shape[0]), jnp.float32)
    for number in range(count):
        panel = sku_unit[number * width : (number + 1) * width]
        block_probe = probe_cols[number * width : (number + 1) * width]
        corr = lax.dot_general(
            piece, panel, (((1,), (1,)), ((), ())), preferred_element_type=jnp.float32
        )
        affinity = jnp.exp(corr).astype(jnp.bfloat16)
        total = total + lax.dot_general(
            block_probe, affinity, (((0,), (1,)), ((), ())), preferred_element_type=jnp.float32
        )
    image = lax.psum_scatter(total, "col", scatter_dimension=1, tiled=True)
    local_gram = jnp.dot(image * demand_weight, image.T, precision=lax.Precision.HIGHEST)
    gram = lax.psum(local_gram, ("row", "col"))
    lower = jnp.linalg.cholesky(gram)
    return jax.scipy.linalg.solve_triangular(lower, image, lower=True)


def other(place, step):
    low = (place % 2 + step % 2) % 2
    high = (place // 2 + step // 2) % 2
    return 2 * high + low


def remote(source, target, sent, landed, row, col):
    return pltpu.make_async_remote_copy(
        src_ref=source,
        dst_ref=target,
        send_sem=sent,
        recv_sem=landed,
        device_id=(row, col),
        device_id_type=pl.DeviceIdType.MESH,
    )


def fused(
    strip_hbm, sku_ref, probe_hbm, weight_hbm, out_ref,
    strip_ref, probe_ref, weight_ref, raw, probe_raw, probe_stage, probe_wide, full, units, strips, partial, arrived, gram_line, gram_group,
    sku_sent, sku_landed, probe_sent, probe_landed, strip_sent, strip_landed,
    pair_sent, pair_landed, twin_sent, twin_landed, image_sent, image_landed,
    line_sent, line_landed, group_sent, group_landed, loaded,
):
    row, col = lax.axis_index("row"), lax.axis_index("col")
    core = row % 2
    z, y = col // 2, col % 2
    twin = row + 1 - 2 * core
    mate = col + 1 - 2 * y
    part, skus = sku_ref.shape
    columns = probe_ref.shape[0]
    loads = [
        pltpu.make_async_copy(source, target, loaded.at[number])
        for number, (source, target) in enumerate(
            ((strip_hbm, strip_ref), (probe_hbm, probe_ref), (weight_hbm, weight_ref), (sku_ref, raw.at[row]))
        )
    ]
    for load in loads:
        load.start()
    factors = ROWS * part
    block = ROWS * columns
    half = skus // 2
    fold = skus // ROWS

    def line_col(place):
        return place * 2 + y

    barrier = pltpu.get_barrier_semaphore()
    for step in range(1, ROWS):
        pl.semaphore_signal(barrier, inc=1, device_id=(other(row, step), col), device_id_type=pl.DeviceIdType.MESH)
    for step in range(1, LINE):
        pl.semaphore_signal(barrier, inc=1, device_id=(row, line_col(other(z, step))), device_id_type=pl.DeviceIdType.MESH)
    for step in range(ROWS):
        pl.semaphore_signal(barrier, inc=1, device_id=(other(row, step), mate), device_id_type=pl.DeviceIdType.MESH)

    sends = []

    def send(copy):
        copy.start()
        sends.append(copy)

    def sku_copy(side, step, there, slot):
        lanes = slice(side * half, (side + 1) * half)
        return remote(
            sku_ref.at[:, lanes], raw.at[slot, :, lanes], sku_sent.at[side, step], sku_landed.at[side, slot], there, col
        )

    pl.semaphore_wait(barrier, 2 * ROWS + LINE - 2)

    for step in (2, 3, 1):
        send(sku_copy(0, step, other(row, step), row))
    loads[1].wait()
    for piece in range(ROWS):
        probe_stage[piece * columns : (piece + 1) * columns, :] = probe_ref[
            :, piece * fold : (piece + 1) * fold
        ].astype(jnp.float32)
    probe_raw[row] = probe_stage[...].astype(jnp.bfloat16)
    for step in (2, 3, 1):
        there = other(row, step)
        send(remote(probe_raw.at[row], probe_raw.at[row], probe_sent.at[step], probe_landed.at[row], there, col))
    for step in (2, 3, 1):
        send(sku_copy(1, step, other(row, step), row))
    loads[0].wait()
    wide = strip_ref[...].astype(jnp.float32)
    scale = lax.rsqrt(jnp.sum(wide * wide, axis=0, keepdims=True) + 1e-06)
    strips[z] = (wide * scale).astype(jnp.bfloat16)
    for step in range(1, LINE):
        there = line_col(other(z, step))
        send(remote(strips.at[z], strips.at[z], strip_sent.at[step], strip_landed.at[z], row, there))

    loads[3].wait()
    for step in range(1, ROWS):
        there = other(row, step)
        remote(
            probe_raw.at[there], probe_raw.at[there], probe_sent.at[step], probe_landed.at[there], there, col
        ).wait_recv()
    for there in range(ROWS):
        folded = probe_raw[there].astype(jnp.float32)
        for piece in range(ROWS):
            probe_wide[there * columns : (there + 1) * columns, piece * fold : (piece + 1) * fold] = folded[
                piece * columns : (piece + 1) * columns
            ]

    pair = remote(full.at[0, core], full.at[1, core], pair_sent, pair_landed, row, mate)
    relay = remote(full.at[1, core], full.at[1, core], twin_sent, twin_landed, twin, col)

    def strip_wait(place, step):
        remote(
            strips.at[place], strips.at[place], strip_sent.at[step], strip_landed.at[place], row, line_col(place)
        ).wait_recv()

    def image_blocks(tasks):
        steps = [(number, first) for number in range(len(tasks)) for first in range(0, half, CHUNK)]
        totals = [jnp.zeros((block, strips.shape[2]), jnp.float32) for _ in tasks]
        corr = affinity = None
        for turn in range(len(steps) + 2):
            corr_next = affinity_next = None
            if turn < len(steps):
                number, first = steps[turn]
                which, side, place = tasks[number]
                corr_next = jnp.dot(
                    units[which, side, first : first + CHUNK, :], strips[place], preferred_element_type=jnp.float32
                )
            if corr is not None:
                affinity_next = jnp.exp2(corr * LOG2_E).astype(jnp.bfloat16)
            if affinity is not None:
                number, first = steps[turn - 2]
                which, side, place = tasks[number]
                totals[number] = totals[number] + jnp.dot(
                    full[which, side, factors:, first : first + CHUNK], affinity, preferred_element_type=jnp.float32
                )
            corr, affinity = corr_next, affinity_next
        return totals

    def image_block(which, side, place):
        return image_blocks([(which, side, place)])[0]

    for side in range(2):
        for step in range(1, ROWS):
            there = other(row, step)
            sku_copy(side, step, there, there).wait_recv()
        lanes = slice(side * half, (side + 1) * half)
        wide = raw[:, :, lanes].reshape(factors, half).astype(jnp.float32)
        scale = lax.rsqrt(jnp.sum(wide * wide, axis=0, keepdims=True) + 1e-06)
        unit = (wide * scale).astype(jnp.bfloat16)
        full[0, side, 0:factors, :] = unit
        full[0, side, factors:, :] = probe_wide[:, lanes].astype(jnp.bfloat16)
        units[0, side] = unit.T

        @pl.when(core == side)
        def _():
            pair.start()

        if side == 0:
            partial[z] = image_block(0, 0, z)
            near = other(z, 1)
            strip_wait(near, 1)
            partial[near] = image_block(0, 0, near)
        else:
            for place, total in zip((z, near), image_blocks([(0, 1, z), (0, 1, near)])):
                partial[place] += total

    def farther(step, carry):
        place = other(z, step)
        strip_wait(place, step)
        partial[place] = sum(image_blocks([(0, 0, place), (0, 1, place)]))
        return carry

    lax.fori_loop(2, LINE, farther, 0)

    places = [other(z, step) for step in range(1, LINE)]
    pair.wait_recv()
    relay.start()
    units[1, core] = full[1, core, 0:factors, :].T

    for place, total in zip(places, image_blocks([(1, core, place) for place in places])):
        partial[place] += total

    last = 1 - core
    remote(full.at[1, last], full.at[1, last], twin_sent, twin_landed, twin, col).wait_recv()
    units[1, last] = full[1, last, 0:factors, :].T

    def mate_last(step, carry):
        place = other(z, LINE - 1 - step)
        partial[place] += image_block(1, last, place)

        remote(
            partial.at[place], arrived.at[z], image_sent.at[step], image_landed.at[z], row, line_col(place)
        ).start()
        return carry

    lax.fori_loop(0, LINE - 1, mate_last, 0)

    image = partial[z] + sum(image_blocks([(1, 0, z), (1, 1, z)]))
    for step in range(1, LINE):
        place = other(z, step)
        remote(
            partial.at[place], arrived.at[place], image_sent.at[step], image_landed.at[place], row, line_col(place)
        ).wait_recv()
        image = image + arrived[place]

    loads[2].wait()
    local = lax.dot_general(
        image * weight_ref[...], image, (((1,), (1,)), ((), ())),
        precision=lax.Precision.HIGHEST, preferred_element_type=jnp.float32,
    )
    gram_line[z] = jnp.zeros(gram_line.shape[1:], jnp.float32)
    gram_line[z, :, 0:block] = local
    for step in range(1, LINE):
        there = line_col(other(z, step))
        send(remote(gram_line.at[z], gram_line.at[z], line_sent.at[step], line_landed.at[z], row, there))
    for step in range(1, LINE):
        place = other(z, step)
        remote(
            gram_line.at[place], gram_line.at[place], line_sent.at[step], line_landed.at[place], row, line_col(place)
        ).wait_recv()
    mine = row * 2 + y
    gram_group[mine] = (gram_line[0] + gram_line[1]) + (gram_line[2] + gram_line[3])
    for step in range(1, GROUP):
        there_row, there_y = other(row, step // 2), (y + step % 2) % 2
        send(
            remote(
                gram_group.at[mine], gram_group.at[mine], group_sent.at[step], group_landed.at[mine],
                there_row, z * 2 + there_y,
            )
        )
    for step in range(1, GROUP):
        there_row, there_y = other(row, step // 2), (y + step % 2) % 2
        slot = there_row * 2 + there_y
        remote(
            gram_group.at[slot], gram_group.at[slot], group_sent.at[step], group_landed.at[slot],
            there_row, z * 2 + there_y,
        ).wait_recv()
    gram = gram_group[0]
    for slot in range(1, GROUP):
        gram = gram + gram_group[slot]

    lanes = 128
    rank = lax.broadcasted_iota(jnp.int32, (block, lanes), 0)
    pivots = [jnp.broadcast_to(gram[:, k : k + 1], (block, lanes)) for k in range(block)]
    pieces = [image[:, left : left + lanes] for left in range(0, image.shape[1], lanes)]
    diagonal = jnp.ones((block, lanes), jnp.float32)
    for k in range(block):
        pivot = pivots[k][k : k + 1, :]
        diagonal = jnp.where(rank == k, pivot, diagonal)
        if k < block - 1:
            factor = jnp.where(rank > k, pivots[k] * (1.0 / pivot), 0.0)
            for later in range(k + 1, block):
                pivots[later] = pivots[later] - factor * pivots[later][k : k + 1, :]
            pieces = [piece - factor * piece[k : k + 1, :] for piece in pieces]
    root = lax.rsqrt(diagonal)
    for number, piece in enumerate(pieces):
        out_ref[:, number * lanes : (number + 1) * lanes] = piece * root

    for copy in sends:
        copy.wait_send()
    pair.wait_send()
    relay.wait_send()
    for step in range(LINE - 1):
        remote(partial.at[z], arrived.at[z], image_sent.at[step], image_landed.at[z], row, mate).wait_send()


def fused_per_device(strip_factors, sku_factors, probe, demand_weight):
    strip, factors = strip_factors.shape
    skus, part = sku_factors.shape
    columns = probe.shape[1]
    block = ROWS * columns
    bf16, f32 = jnp.bfloat16, jnp.float32
    dma = pltpu.SemaphoreType.DMA
    whole = pl.BlockSpec(memory_space=pltpu.VMEM)
    far = pl.BlockSpec(memory_space=pltpu.HBM)
    return pl.pallas_call(
        fused,
        out_shape=pltpu.VMEM((block, strip), f32),
        in_specs=[far] * 4,
        out_specs=whole,
        scratch_shapes=[
            pltpu.VMEM((factors, strip), bf16),
            pltpu.VMEM((columns, skus), bf16),
            pltpu.VMEM((1, strip), f32),
            pltpu.VMEM((ROWS, part, skus), bf16),
            pltpu.VMEM((ROWS, block, skus // ROWS), bf16),
            pltpu.VMEM((block, skus // ROWS), f32),
            pltpu.VMEM((block, skus), f32),
            pltpu.VMEM((2, 2, factors + block, skus // 2), bf16),
            pltpu.VMEM((2, 2, skus // 2, factors), bf16),
            pltpu.VMEM((LINE, factors, strip), bf16),
            pltpu.VMEM((LINE, block, strip), f32),
            pltpu.VMEM((LINE, block, strip), f32),
            pltpu.VMEM((LINE, block, 128), f32),
            pltpu.VMEM((GROUP, block, 128), f32),
        ]
        + [dma((2, ROWS))] * 2 + [dma((ROWS,))] * 2 + [dma((LINE,))] * 2 + [dma] * 4 + [dma((LINE,))] * 4 + [dma((GROUP,))] * 2 + [dma((4,))],
        compiler_params=pltpu.CompilerParams(
            collective_id=0, has_side_effects=True, vmem_limit_bytes=60 * 1024 * 1024
        ),
        cost_estimate=pl.CostEstimate(
            flops=2 * LINE * strip * 2 * skus * (factors + block),
            bytes_accessed=2 * (strip * factors + skus * part + skus * columns) + 4 * block * strip,
            transcendentals=LINE * strip * 2 * skus,
        ),
    )(strip_factors.T, sku_factors.T, probe.T, demand_weight)


def fits(mesh):
    return mesh.shape["row"] == ROWS and mesh.shape["col"] == 2 * LINE


def solution(mesh):
    placed = (P(("row", "col"), None), P("col", "row"), P("col", "row"), P(None, ("row", "col")))
    plan = fused_per_device if fits(mesh) else per_device
    return jax.shard_map(
        plan, mesh=mesh, in_specs=placed, out_specs=P(None, ("row", "col")), check_vma=False
    )
```

```python
import jax
import jax.numpy as jnp
from jax import lax
from jax.experimental import pallas as pl
from jax.experimental.pallas import tpu as pltpu
from jax.sharding import PartitionSpec as P

ROWS = 4
LINE = 4
GROUP = 2 * ROWS
CHUNK = 512
LOG2_E = 1.4426950408889634


def unit_rows(factors):
    wide = factors.astype(jnp.float32)
    scale = lax.rsqrt(jnp.sum(wide * wide, axis=1, keepdims=True) + 1e-06)
    return (wide * scale).astype(jnp.bfloat16)


def per_device(strip_factors, sku_factors, probe, demand_weight):
    strip_unit = unit_rows(strip_factors)
    panel_raw, probe_cols = (
        lax.all_gather(sku_factors, "row", axis=1, tiled=True),
        lax.all_gather(probe, "row", axis=1, tiled=True),
    )
    sku_unit = unit_rows(panel_raw)
    columns = sku_unit.shape[0]
    width = min(512, columns)
    count = columns // width
    piece = lax.all_gather(strip_unit, "col", axis=0, tiled=True)
    total = jnp.zeros((probe_cols.shape[1], piece.shape[0]), jnp.float32)
    for number in range(count):
        panel = sku_unit[number * width : (number + 1) * width]
        block_probe = probe_cols[number * width : (number + 1) * width]
        corr = lax.dot_general(
            piece, panel, (((1,), (1,)), ((), ())), preferred_element_type=jnp.float32
        )
        affinity = jnp.exp(corr).astype(jnp.bfloat16)
        total = total + lax.dot_general(
            block_probe, affinity, (((0,), (1,)), ((), ())), preferred_element_type=jnp.float32
        )
    image = lax.psum_scatter(total, "col", scatter_dimension=1, tiled=True)
    local_gram = jnp.dot(image * demand_weight, image.T, precision=lax.Precision.HIGHEST)
    gram = lax.psum(local_gram, ("row", "col"))
    lower = jnp.linalg.cholesky(gram)
    return jax.scipy.linalg.solve_triangular(lower, image, lower=True)


def other(place, step):
    low = (place % 2 + step % 2) % 2
    high = (place // 2 + step // 2) % 2
    return 2 * high + low


def remote(source, target, sent, landed, row, col):
    return pltpu.make_async_remote_copy(
        src_ref=source,
        dst_ref=target,
        send_sem=sent,
        recv_sem=landed,
        device_id=(row, col),
        device_id_type=pl.DeviceIdType.MESH,
    )


def fused(
    strip_hbm, sku_ref, probe_hbm, weight_hbm, out_ref,
    strip_ref, probe_ref, weight_ref, raw, probe_raw, probe_stage, probe_wide, full, units, strips, partial, arrived, gram_line, gram_group,
    sku_sent, sku_landed, probe_sent, probe_landed, strip_sent, strip_landed,
    pair_sent, pair_landed, twin_sent, twin_landed, image_sent, image_landed,
    line_sent, line_landed, group_sent, group_landed, loaded,
):
    row, col = lax.axis_index("row"), lax.axis_index("col")
    core = row % 2
    z, y = col // 2, col % 2
    twin = row + 1 - 2 * core
    mate = col + 1 - 2 * y
    part, skus = sku_ref.shape
    columns = probe_ref.shape[0]
    loads = [
        pltpu.make_async_copy(source, target, loaded.at[number])
        for number, (source, target) in enumerate(
            ((strip_hbm, strip_ref), (probe_hbm, probe_ref), (weight_hbm, weight_ref), (sku_ref, raw.at[row]))
        )
    ]
    for load in loads:
        load.start()
    factors = ROWS * part
    block = ROWS * columns
    half = skus // 2
    fold = skus // ROWS

    def line_col(place):
        return place * 2 + y

    barrier = pltpu.get_barrier_semaphore()
    for step in range(1, ROWS):
        pl.semaphore_signal(barrier, inc=1, device_id=(other(row, step), col), device_id_type=pl.DeviceIdType.MESH)
    for step in range(1, LINE):
        pl.semaphore_signal(barrier, inc=1, device_id=(row, line_col(other(z, step))), device_id_type=pl.DeviceIdType.MESH)
    for step in range(ROWS):
        pl.semaphore_signal(barrier, inc=1, device_id=(other(row, step), mate), device_id_type=pl.DeviceIdType.MESH)

    sends = []

    def send(copy):
        copy.start()
        sends.append(copy)

    def sku_copy(side, step, there, slot):
        lanes = slice(side * half, (side + 1) * half)
        return remote(
            sku_ref.at[:, lanes], raw.at[slot, :, lanes], sku_sent.at[side, step], sku_landed.at[side, slot], there, col
        )

    pl.semaphore_wait(barrier, 2 * ROWS + LINE - 2)

    for step in (2, 3, 1):
        send(sku_copy(0, step, other(row, step), row))
    loads[1].wait()
    for piece in range(ROWS):
        probe_stage[piece * columns : (piece + 1) * columns, :] = probe_ref[
            :, piece * fold : (piece + 1) * fold
        ].astype(jnp.float32)
    probe_raw[row] = probe_stage[...].astype(jnp.bfloat16)
    for step in (2, 3, 1):
        there = other(row, step)
        send(remote(probe_raw.at[row], probe_raw.at[row], probe_sent.at[step], probe_landed.at[row], there, col))
    for step in (2, 3, 1):
        send(sku_copy(1, step, other(row, step), row))
    loads[0].wait()
    wide = strip_ref[...].astype(jnp.float32)
    scale = lax.rsqrt(jnp.sum(wide * wide, axis=0, keepdims=True) + 1e-06)
    strips[z] = (wide * scale).astype(jnp.bfloat16)
    for step in range(1, LINE):
        there = line_col(other(z, step))
        send(remote(strips.at[z], strips.at[z], strip_sent.at[step], strip_landed.at[z], row, there))

    loads[3].wait()
    for step in range(1, ROWS):
        there = other(row, step)
        remote(
            probe_raw.at[there], probe_raw.at[there], probe_sent.at[step], probe_landed.at[there], there, col
        ).wait_recv()
    for there in range(ROWS):
        folded = probe_raw[there].astype(jnp.float32)
        for piece in range(ROWS):
            probe_wide[there * columns : (there + 1) * columns, piece * fold : (piece + 1) * fold] = folded[
                piece * columns : (piece + 1) * columns
            ]

    pair = remote(full.at[0, core], full.at[1, core], pair_sent, pair_landed, row, mate)
    relay = remote(full.at[1, core], full.at[1, core], twin_sent, twin_landed, twin, col)

    def strip_wait(place, step):
        remote(
            strips.at[place], strips.at[place], strip_sent.at[step], strip_landed.at[place], row, line_col(place)
        ).wait_recv()

    def image_blocks(tasks):
        steps = [(number, first) for number in range(len(tasks)) for first in range(0, half, CHUNK)]
        totals = [jnp.zeros((block, strips.shape[2]), jnp.float32) for _ in tasks]
        corr = affinity = None
        for turn in range(len(steps) + 2):
            corr_next = affinity_next = None
            if turn < len(steps):
                number, first = steps[turn]
                which, side, place = tasks[number]
                corr_next = jnp.dot(
                    units[which, side, first : first + CHUNK, :], strips[place], preferred_element_type=jnp.float32
                )
            if corr is not None:
                affinity_next = jnp.exp2(corr * LOG2_E).astype(jnp.bfloat16)
            if affinity is not None:
                number, first = steps[turn - 2]
                which, side, place = tasks[number]
                totals[number] = totals[number] + jnp.dot(
                    full[which, side, factors:, first : first + CHUNK], affinity, preferred_element_type=jnp.float32
                )
            corr, affinity = corr_next, affinity_next
        return totals

    def image_block(which, side, place):
        return image_blocks([(which, side, place)])[0]

    for side in range(2):
        for step in range(1, ROWS):
            there = other(row, step)
            sku_copy(side, step, there, there).wait_recv()
        lanes = slice(side * half, (side + 1) * half)
        wide = raw[:, :, lanes].reshape(factors, half).astype(jnp.float32)
        scale = lax.rsqrt(jnp.sum(wide * wide, axis=0, keepdims=True) + 1e-06)
        unit = (wide * scale).astype(jnp.bfloat16)
        full[0, side, 0:factors, :] = unit
        full[0, side, factors:, :] = probe_wide[:, lanes].astype(jnp.bfloat16)
        units[0, side] = unit.T

        @pl.when(core == side)
        def _():
            pair.start()

        if side == 0:
            partial[z] = image_block(0, 0, z)
            near = other(z, 1)
            strip_wait(near, 1)
            partial[near] = image_block(0, 0, near)
        else:
            for place, total in zip((z, near), image_blocks([(0, 1, z), (0, 1, near)])):
                partial[place] += total

    def farther(step, carry):
        place = other(z, step)
        strip_wait(place, step)
        partial[place] = sum(image_blocks([(0, 0, place), (0, 1, place)]))
        return carry

    lax.fori_loop(2, LINE, farther, 0)

    places = [other(z, step) for step in range(1, LINE)]
    pair.wait_recv()
    relay.start()
    units[1, core] = full[1, core, 0:factors, :].T

    for place, total in zip(places, image_blocks([(1, core, place) for place in places])):
        partial[place] += total

    last = 1 - core
    remote(full.at[1, last], full.at[1, last], twin_sent, twin_landed, twin, col).wait_recv()
    units[1, last] = full[1, last, 0:factors, :].T

    def mate_last(step, carry):
        place = other(z, LINE - 1 - step)
        partial[place] += image_block(1, last, place)

        remote(
            partial.at[place], arrived.at[z], image_sent.at[step], image_landed.at[z], row, line_col(place)
        ).start()
        return carry

    lax.fori_loop(0, LINE - 1, mate_last, 0)

    image = partial[z] + sum(image_blocks([(1, 0, z), (1, 1, z)]))
    for step in range(1, LINE):
        place = other(z, step)
        remote(
            partial.at[place], arrived.at[place], image_sent.at[step], image_landed.at[place], row, line_col(place)
        ).wait_recv()
        image = image + arrived[place]

    loads[2].wait()
    local = lax.dot_general(
        image * weight_ref[...], image, (((1,), (1,)), ((), ())),
        precision=lax.Precision.HIGHEST, preferred_element_type=jnp.float32,
    )
    gram_line[z] = jnp.zeros(gram_line.shape[1:], jnp.float32)
    gram_line[z, :, 0:block] = local
    for step in range(1, LINE):
        there = line_col(other(z, step))
        send(remote(gram_line.at[z], gram_line.at[z], line_sent.at[step], line_landed.at[z], row, there))
    for step in range(1, LINE):
        place = other(z, step)
        remote(
            gram_line.at[place], gram_line.at[place], line_sent.at[step], line_landed.at[place], row, line_col(place)
        ).wait_recv()
    mine = row * 2 + y
    gram_group[mine] = (gram_line[0] + gram_line[1]) + (gram_line[2] + gram_line[3])
    for step in range(1, GROUP):
        there_row, there_y = other(row, step // 2), (y + step % 2) % 2
        send(
            remote(
                gram_group.at[mine], gram_group.at[mine], group_sent.at[step], group_landed.at[mine],
                there_row, z * 2 + there_y,
            )
        )
    for step in range(1, GROUP):
        there_row, there_y = other(row, step // 2), (y + step % 2) % 2
        slot = there_row * 2 + there_y
        remote(
            gram_group.at[slot], gram_group.at[slot], group_sent.at[step], group_landed.at[slot],
            there_row, z * 2 + there_y,
        ).wait_recv()
    gram = gram_group[0]
    for slot in range(1, GROUP):
        gram = gram + gram_group[slot]

    lanes = 128
    rank = lax.broadcasted_iota(jnp.int32, (block, lanes), 0)
    pivots = [jnp.broadcast_to(gram[:, k : k + 1], (block, lanes)) for k in range(block)]
    pieces = [image[:, left : left + lanes] for left in range(0, image.shape[1], lanes)]
    diagonal = jnp.ones((block, lanes), jnp.float32)
    for k in range(block):
        pivot = pivots[k][k : k + 1, :]
        diagonal = jnp.where(rank == k, pivot, diagonal)
        if k < block - 1:
            factor = jnp.where(rank > k, pivots[k] * (1.0 / pivot), 0.0)
            for later in range(k + 1, block):
                pivots[later] = pivots[later] - factor * pivots[later][k : k + 1, :]
            pieces = [piece - factor * piece[k : k + 1, :] for piece in pieces]
    root = lax.rsqrt(diagonal)
    for number, piece in enumerate(pieces):
        out_ref[:, number * lanes : (number + 1) * lanes] = piece * root

    for copy in sends:
        copy.wait_send()
    pair.wait_send()
    relay.wait_send()
    for step in range(LINE - 1):
        remote(partial.at[z], arrived.at[z], image_sent.at[step], image_landed.at[z], row, mate).wait_send()


def fused_per_device(strip_factors, sku_factors, probe, demand_weight):
    strip, factors = strip_factors.shape
    skus, part = sku_factors.shape
    columns = probe.shape[1]
    block = ROWS * columns
    bf16, f32 = jnp.bfloat16, jnp.float32
    dma = pltpu.SemaphoreType.DMA
    whole = pl.BlockSpec(memory_space=pltpu.VMEM)
    far = pl.BlockSpec(memory_space=pltpu.HBM)
    return pl.pallas_call(
        fused,
        out_shape=pltpu.VMEM((block, strip), f32),
        in_specs=[far] * 4,
        out_specs=whole,
        scratch_shapes=[
            pltpu.VMEM((factors, strip), bf16),
            pltpu.VMEM((columns, skus), bf16),
            pltpu.VMEM((1, strip), f32),
            pltpu.VMEM((ROWS, part, skus), bf16),
            pltpu.VMEM((ROWS, block, skus // ROWS), bf16),
            pltpu.VMEM((block, skus // ROWS), f32),
            pltpu.VMEM((block, skus), f32),
            pltpu.VMEM((2, 2, factors + block, skus // 2), bf16),
            pltpu.VMEM((2, 2, skus // 2, factors), bf16),
            pltpu.VMEM((LINE, factors, strip), bf16),
            pltpu.VMEM((LINE, block, strip), f32),
            pltpu.VMEM((LINE, block, strip), f32),
            pltpu.VMEM((LINE, block, 128), f32),
            pltpu.VMEM((GROUP, block, 128), f32),
        ]
        + [dma((2, ROWS))] * 2 + [dma((ROWS,))] * 2 + [dma((LINE,))] * 2 + [dma] * 4 + [dma((LINE,))] * 4 + [dma((GROUP,))] * 2 + [dma((4,))],
        compiler_params=pltpu.CompilerParams(
            collective_id=0, has_side_effects=True, vmem_limit_bytes=60 * 1024 * 1024
        ),
        cost_estimate=pl.CostEstimate(
            flops=2 * LINE * strip * 2 * skus * (factors + block),
            bytes_accessed=2 * (strip * factors + skus * part + skus * columns) + 4 * block * strip,
            transcendentals=LINE * strip * 2 * skus,
        ),
    )(strip_factors.T, sku_factors.T, probe.T, demand_weight)


def fits(mesh):
    return mesh.shape["row"] == ROWS and mesh.shape["col"] == 2 * LINE


def solution(mesh):
    placed = (P(("row", "col"), None), P("col", "row"), P("col", "row"), P(None, ("row", "col")))
    plan = fused_per_device if fits(mesh) else per_device
    return jax.shard_map(
        plan, mesh=mesh, in_specs=placed, out_specs=P(None, ("row", "col")), check_vma=False
    )
```

```python
import jax
import jax.numpy as jnp
from jax import lax
from jax.experimental import pallas as pl
from jax.experimental.pallas import tpu as pltpu
from jax.sharding import PartitionSpec as P

ROWS = 4
LINE = 4
GROUP = 2 * ROWS
CHUNK = 256
LOG2_E = 1.4426950408889634


def unit_rows(factors):
    wide = factors.astype(jnp.float32)
    scale = lax.rsqrt(jnp.sum(wide * wide, axis=1, keepdims=True) + 1e-06)
    return (wide * scale).astype(jnp.bfloat16)


def per_device(strip_factors, sku_factors, probe, demand_weight):
    strip_unit = unit_rows(strip_factors)
    panel_raw, probe_cols = (
        lax.all_gather(sku_factors, "row", axis=1, tiled=True),
        lax.all_gather(probe, "row", axis=1, tiled=True),
    )
    sku_unit = unit_rows(panel_raw)
    columns = sku_unit.shape[0]
    width = min(512, columns)
    count = columns // width
    piece = lax.all_gather(strip_unit, "col", axis=0, tiled=True)
    total = jnp.zeros((probe_cols.shape[1], piece.shape[0]), jnp.float32)
    for number in range(count):
        panel = sku_unit[number * width : (number + 1) * width]
        block_probe = probe_cols[number * width : (number + 1) * width]
        corr = lax.dot_general(
            piece, panel, (((1,), (1,)), ((), ())), preferred_element_type=jnp.float32
        )
        affinity = jnp.exp(corr).astype(jnp.bfloat16)
        total = total + lax.dot_general(
            block_probe, affinity, (((0,), (1,)), ((), ())), preferred_element_type=jnp.float32
        )
    image = lax.psum_scatter(total, "col", scatter_dimension=1, tiled=True)
    local_gram = jnp.dot(image * demand_weight, image.T, precision=lax.Precision.HIGHEST)
    gram = lax.psum(local_gram, ("row", "col"))
    lower = jnp.linalg.cholesky(gram)
    return jax.scipy.linalg.solve_triangular(lower, image, lower=True)


def other(place, step):
    low = (place % 2 + step % 2) % 2
    high = (place // 2 + step // 2) % 2
    return 2 * high + low


def remote(source, target, sent, landed, row, col):
    return pltpu.make_async_remote_copy(
        src_ref=source,
        dst_ref=target,
        send_sem=sent,
        recv_sem=landed,
        device_id=(row, col),
        device_id_type=pl.DeviceIdType.MESH,
    )


def fused(
    strip_hbm, sku_ref, probe_hbm, weight_hbm, out_ref,
    strip_ref, probe_ref, weight_ref, raw, probe_raw, probe_stage, probe_wide, full, units, strips, partial, arrived, gram_line, gram_group,
    sku_sent, sku_landed, probe_sent, probe_landed, strip_sent, strip_landed,
    pair_sent, pair_landed, twin_sent, twin_landed, image_sent, image_landed,
    line_sent, line_landed, group_sent, group_landed, loaded,
):
    row, col = lax.axis_index("row"), lax.axis_index("col")
    core = row % 2
    z, y = col // 2, col % 2
    twin = row + 1 - 2 * core
    mate = col + 1 - 2 * y
    part, skus = sku_ref.shape
    columns = probe_ref.shape[0]
    loads = [
        pltpu.make_async_copy(source, target, loaded.at[number])
        for number, (source, target) in enumerate(
            ((strip_hbm, strip_ref), (probe_hbm, probe_ref), (weight_hbm, weight_ref), (sku_ref, raw.at[row]))
        )
    ]
    for load in loads:
        load.start()
    factors = ROWS * part
    block = ROWS * columns
    half = skus // 2
    fold = skus // ROWS

    def line_col(place):
        return place * 2 + y

    barrier = pltpu.get_barrier_semaphore()
    for step in range(1, ROWS):
        pl.semaphore_signal(barrier, inc=1, device_id=(other(row, step), col), device_id_type=pl.DeviceIdType.MESH)
    for step in range(1, LINE):
        pl.semaphore_signal(barrier, inc=1, device_id=(row, line_col(other(z, step))), device_id_type=pl.DeviceIdType.MESH)
    for step in range(ROWS):
        pl.semaphore_signal(barrier, inc=1, device_id=(other(row, step), mate), device_id_type=pl.DeviceIdType.MESH)

    sends = []

    def send(copy):
        copy.start()
        sends.append(copy)

    def sku_copy(side, step, there, slot):
        lanes = slice(side * half, (side + 1) * half)
        return remote(
            sku_ref.at[:, lanes], raw.at[slot, :, lanes], sku_sent.at[side, step], sku_landed.at[side, slot], there, col
        )

    pl.semaphore_wait(barrier, 2 * ROWS + LINE - 2)

    for step in (2, 3, 1):
        send(sku_copy(0, step, other(row, step), row))
    loads[1].wait()
    for piece in range(ROWS):
        probe_stage[piece * columns : (piece + 1) * columns, :] = probe_ref[
            :, piece * fold : (piece + 1) * fold
        ].astype(jnp.float32)
    probe_raw[row] = probe_stage[...].astype(jnp.bfloat16)
    for step in (2, 3, 1):
        there = other(row, step)
        send(remote(probe_raw.at[row], probe_raw.at[row], probe_sent.at[step], probe_landed.at[row], there, col))
    for step in (2, 3, 1):
        send(sku_copy(1, step, other(row, step), row))
    loads[0].wait()
    wide = strip_ref[...].astype(jnp.float32)
    scale = lax.rsqrt(jnp.sum(wide * wide, axis=0, keepdims=True) + 1e-06)
    strips[z] = (wide * scale).astype(jnp.bfloat16)
    for step in range(1, LINE):
        there = line_col(other(z, step))
        send(remote(strips.at[z], strips.at[z], strip_sent.at[step], strip_landed.at[z], row, there))

    loads[3].wait()
    for step in range(1, ROWS):
        there = other(row, step)
        remote(
            probe_raw.at[there], probe_raw.at[there], probe_sent.at[step], probe_landed.at[there], there, col
        ).wait_recv()
    for there in range(ROWS):
        folded = probe_raw[there].astype(jnp.float32)
        for piece in range(ROWS):
            probe_wide[there * columns : (there + 1) * columns, piece * fold : (piece + 1) * fold] = folded[
                piece * columns : (piece + 1) * columns
            ]

    pair = remote(full.at[0, core], full.at[1, core], pair_sent, pair_landed, row, mate)
    relay = remote(full.at[1, core], full.at[1, core], twin_sent, twin_landed, twin, col)

    def strip_wait(place, step):
        remote(
            strips.at[place], strips.at[place], strip_sent.at[step], strip_landed.at[place], row, line_col(place)
        ).wait_recv()

    def image_blocks(tasks):
        wide = strips.shape[2]
        steps = [
            (number, first, left)
            for number in range(len(tasks))
            for first in range(0, half, CHUNK)
            for left in range(0, wide, CHUNK)
        ]
        totals = {
            (number, left): jnp.zeros((block, CHUNK), jnp.float32)
            for number in range(len(tasks))
            for left in range(0, wide, CHUNK)
        }
        corr = affinity = None
        for turn in range(len(steps) + 2):
            corr_next = affinity_next = None
            if turn < len(steps):
                number, first, left = steps[turn]
                which, side, place = tasks[number]
                corr_next = jnp.dot(
                    units[which, side, first : first + CHUNK, :], strips[place, :, left : left + CHUNK],
                    preferred_element_type=jnp.float32,
                )
            if corr is not None:
                affinity_next = jnp.exp2(corr * LOG2_E).astype(jnp.bfloat16)
            if affinity is not None:
                number, first, left = steps[turn - 2]
                which, side, place = tasks[number]
                totals[number, left] = totals[number, left] + jnp.dot(
                    full[which, side, factors:, first : first + CHUNK], affinity, preferred_element_type=jnp.float32
                )
            corr, affinity = corr_next, affinity_next
        return [
            jnp.concatenate([totals[number, left] for left in range(0, wide, CHUNK)], axis=1)
            for number in range(len(tasks))
        ]

    def image_block(which, side, place):
        return image_blocks([(which, side, place)])[0]

    for side in range(2):
        for step in range(1, ROWS):
            there = other(row, step)
            sku_copy(side, step, there, there).wait_recv()
        lanes = slice(side * half, (side + 1) * half)
        wide = raw[:, :, lanes].reshape(factors, half).astype(jnp.float32)
        scale = lax.rsqrt(jnp.sum(wide * wide, axis=0, keepdims=True) + 1e-06)
        unit = (wide * scale).astype(jnp.bfloat16)
        full[0, side, 0:factors, :] = unit
        full[0, side, factors:, :] = probe_wide[:, lanes].astype(jnp.bfloat16)
        units[0, side] = unit.T

        @pl.when(core == side)
        def _():
            pair.start()

        if side == 0:
            partial[z] = image_block(0, 0, z)
            near = other(z, 1)
            strip_wait(near, 1)
            partial[near] = image_block(0, 0, near)
        else:
            for place, total in zip((z, near), image_blocks([(0, 1, z), (0, 1, near)])):
                partial[place] += total

    def farther(step, carry):
        place = other(z, step)
        strip_wait(place, step)
        partial[place] = sum(image_blocks([(0, 0, place), (0, 1, place)]))
        return carry

    lax.fori_loop(2, LINE, farther, 0)

    places = [other(z, step) for step in range(1, LINE)]
    pair.wait_recv()
    relay.start()
    units[1, core] = full[1, core, 0:factors, :].T

    for place, total in zip(places, image_blocks([(1, core, place) for place in places])):
        partial[place] += total

    last = 1 - core
    remote(full.at[1, last], full.at[1, last], twin_sent, twin_landed, twin, col).wait_recv()
    units[1, last] = full[1, last, 0:factors, :].T

    def mate_last(step, carry):
        place = other(z, LINE - 1 - step)
        partial[place] += image_block(1, last, place)

        remote(
            partial.at[place], arrived.at[z], image_sent.at[step], image_landed.at[z], row, line_col(place)
        ).start()
        return carry

    lax.fori_loop(0, LINE - 1, mate_last, 0)

    image = partial[z] + sum(image_blocks([(1, 0, z), (1, 1, z)]))
    for step in range(1, LINE):
        place = other(z, step)
        remote(
            partial.at[place], arrived.at[place], image_sent.at[step], image_landed.at[place], row, line_col(place)
        ).wait_recv()
        image = image + arrived[place]

    loads[2].wait()
    local = lax.dot_general(
        image * weight_ref[...], image, (((1,), (1,)), ((), ())),
        precision=lax.Precision.HIGHEST, preferred_element_type=jnp.float32,
    )
    gram_line[z] = jnp.zeros(gram_line.shape[1:], jnp.float32)
    gram_line[z, :, 0:block] = local
    for step in range(1, LINE):
        there = line_col(other(z, step))
        send(remote(gram_line.at[z], gram_line.at[z], line_sent.at[step], line_landed.at[z], row, there))
    for step in range(1, LINE):
        place = other(z, step)
        remote(
            gram_line.at[place], gram_line.at[place], line_sent.at[step], line_landed.at[place], row, line_col(place)
        ).wait_recv()
    mine = row * 2 + y
    gram_group[mine] = (gram_line[0] + gram_line[1]) + (gram_line[2] + gram_line[3])
    for step in range(1, GROUP):
        there_row, there_y = other(row, step // 2), (y + step % 2) % 2
        send(
            remote(
                gram_group.at[mine], gram_group.at[mine], group_sent.at[step], group_landed.at[mine],
                there_row, z * 2 + there_y,
            )
        )
    for step in range(1, GROUP):
        there_row, there_y = other(row, step // 2), (y + step % 2) % 2
        slot = there_row * 2 + there_y
        remote(
            gram_group.at[slot], gram_group.at[slot], group_sent.at[step], group_landed.at[slot],
            there_row, z * 2 + there_y,
        ).wait_recv()
    gram = gram_group[0]
    for slot in range(1, GROUP):
        gram = gram + gram_group[slot]

    lanes = 128
    rank = lax.broadcasted_iota(jnp.int32, (block, lanes), 0)
    pivots = [jnp.broadcast_to(gram[:, k : k + 1], (block, lanes)) for k in range(block)]
    pieces = [image[:, left : left + lanes] for left in range(0, image.shape[1], lanes)]
    diagonal = jnp.ones((block, lanes), jnp.float32)
    for k in range(block):
        pivot = pivots[k][k : k + 1, :]
        diagonal = jnp.where(rank == k, pivot, diagonal)
        if k < block - 1:
            factor = jnp.where(rank > k, pivots[k] * (1.0 / pivot), 0.0)
            for later in range(k + 1, block):
                pivots[later] = pivots[later] - factor * pivots[later][k : k + 1, :]
            pieces = [piece - factor * piece[k : k + 1, :] for piece in pieces]
    root = lax.rsqrt(diagonal)
    for number, piece in enumerate(pieces):
        out_ref[:, number * lanes : (number + 1) * lanes] = piece * root

    for copy in sends:
        copy.wait_send()
    pair.wait_send()
    relay.wait_send()
    for step in range(LINE - 1):
        remote(partial.at[z], arrived.at[z], image_sent.at[step], image_landed.at[z], row, mate).wait_send()


def fused_per_device(strip_factors, sku_factors, probe, demand_weight):
    strip, factors = strip_factors.shape
    skus, part = sku_factors.shape
    columns = probe.shape[1]
    block = ROWS * columns
    bf16, f32 = jnp.bfloat16, jnp.float32
    dma = pltpu.SemaphoreType.DMA
    whole = pl.BlockSpec(memory_space=pltpu.VMEM)
    far = pl.BlockSpec(memory_space=pltpu.HBM)
    return pl.pallas_call(
        fused,
        out_shape=pltpu.VMEM((block, strip), f32),
        in_specs=[far] * 4,
        out_specs=whole,
        scratch_shapes=[
            pltpu.VMEM((factors, strip), bf16),
            pltpu.VMEM((columns, skus), bf16),
            pltpu.VMEM((1, strip), f32),
            pltpu.VMEM((ROWS, part, skus), bf16),
            pltpu.VMEM((ROWS, block, skus // ROWS), bf16),
            pltpu.VMEM((block, skus // ROWS), f32),
            pltpu.VMEM((block, skus), f32),
            pltpu.VMEM((2, 2, factors + block, skus // 2), bf16),
            pltpu.VMEM((2, 2, skus // 2, factors), bf16),
            pltpu.VMEM((LINE, factors, strip), bf16),
            pltpu.VMEM((LINE, block, strip), f32),
            pltpu.VMEM((LINE, block, strip), f32),
            pltpu.VMEM((LINE, block, 128), f32),
            pltpu.VMEM((GROUP, block, 128), f32),
        ]
        + [dma((2, ROWS))] * 2 + [dma((ROWS,))] * 2 + [dma((LINE,))] * 2 + [dma] * 4 + [dma((LINE,))] * 4 + [dma((GROUP,))] * 2 + [dma((4,))],
        compiler_params=pltpu.CompilerParams(
            collective_id=0, has_side_effects=True, vmem_limit_bytes=60 * 1024 * 1024
        ),
        cost_estimate=pl.CostEstimate(
            flops=2 * LINE * strip * 2 * skus * (factors + block),
            bytes_accessed=2 * (strip * factors + skus * part + skus * columns) + 4 * block * strip,
            transcendentals=LINE * strip * 2 * skus,
        ),
    )(strip_factors.T, sku_factors.T, probe.T, demand_weight)


def fits(mesh):
    return mesh.shape["row"] == ROWS and mesh.shape["col"] == 2 * LINE


def solution(mesh):
    placed = (P(("row", "col"), None), P("col", "row"), P("col", "row"), P(None, ("row", "col")))
    plan = fused_per_device if fits(mesh) else per_device
    return jax.shard_map(
        plan, mesh=mesh, in_specs=placed, out_specs=P(None, ("row", "col")), check_vma=False
    )
```

```python
import jax
import jax.numpy as jnp
from jax import lax
from jax.experimental import pallas as pl
from jax.experimental.pallas import tpu as pltpu
from jax.sharding import PartitionSpec as P

ROWS = 4
LINE = 4
GROUP = 2 * ROWS
CHUNK = 256
LOG2_E = 1.4426950408889634


def unit_rows(factors):
    wide = factors.astype(jnp.float32)
    scale = lax.rsqrt(jnp.sum(wide * wide, axis=1, keepdims=True) + 1e-06)
    return (wide * scale).astype(jnp.bfloat16)


def per_device(strip_factors, sku_factors, probe, demand_weight):
    strip_unit = unit_rows(strip_factors)
    panel_raw, probe_cols = (
        lax.all_gather(sku_factors, "row", axis=1, tiled=True),
        lax.all_gather(probe, "row", axis=1, tiled=True),
    )
    sku_unit = unit_rows(panel_raw)
    columns = sku_unit.shape[0]
    width = min(512, columns)
    count = columns // width
    piece = lax.all_gather(strip_unit, "col", axis=0, tiled=True)
    total = jnp.zeros((probe_cols.shape[1], piece.shape[0]), jnp.float32)
    for number in range(count):
        panel = sku_unit[number * width : (number + 1) * width]
        block_probe = probe_cols[number * width : (number + 1) * width]
        corr = lax.dot_general(
            piece, panel, (((1,), (1,)), ((), ())), preferred_element_type=jnp.float32
        )
        affinity = jnp.exp(corr).astype(jnp.bfloat16)
        total = total + lax.dot_general(
            block_probe, affinity, (((0,), (1,)), ((), ())), preferred_element_type=jnp.float32
        )
    image = lax.psum_scatter(total, "col", scatter_dimension=1, tiled=True)
    local_gram = jnp.dot(image * demand_weight, image.T, precision=lax.Precision.HIGHEST)
    gram = lax.psum(local_gram, ("row", "col"))
    lower = jnp.linalg.cholesky(gram)
    return jax.scipy.linalg.solve_triangular(lower, image, lower=True)


def other(place, step):
    low = (place % 2 + step % 2) % 2
    high = (place // 2 + step // 2) % 2
    return 2 * high + low


def remote(source, target, sent, landed, row, col):
    return pltpu.make_async_remote_copy(
        src_ref=source,
        dst_ref=target,
        send_sem=sent,
        recv_sem=landed,
        device_id=(row, col),
        device_id_type=pl.DeviceIdType.MESH,
    )


def fused(
    strip_hbm, sku_ref, probe_hbm, weight_hbm, out_ref,
    strip_ref, probe_ref, weight_ref, raw, probe_raw, probe_stage, probe_wide, full, units, strips, partial, arrived, gram_line, gram_group,
    sku_sent, sku_landed, probe_sent, probe_landed, strip_sent, strip_landed,
    pair_sent, pair_landed, twin_sent, twin_landed, image_sent, image_landed,
    line_sent, line_landed, group_sent, group_landed, loaded,
):
    row, col = lax.axis_index("row"), lax.axis_index("col")
    core = row % 2
    z, y = col // 2, col % 2
    twin = row + 1 - 2 * core
    mate = col + 1 - 2 * y
    part, skus = sku_ref.shape
    columns = probe_ref.shape[0]
    loads = [
        pltpu.make_async_copy(source, target, loaded.at[number])
        for number, (source, target) in enumerate(
            ((strip_hbm, strip_ref), (probe_hbm, probe_ref), (weight_hbm, weight_ref), (sku_ref, raw.at[row]))
        )
    ]
    for load in loads:
        load.start()
    factors = ROWS * part
    block = ROWS * columns
    half = skus // 2
    fold = skus // ROWS

    def line_col(place):
        return place * 2 + y

    barrier = pltpu.get_barrier_semaphore()
    for step in range(1, ROWS):
        pl.semaphore_signal(barrier, inc=1, device_id=(other(row, step), col), device_id_type=pl.DeviceIdType.MESH)
    for step in range(1, LINE):
        pl.semaphore_signal(barrier, inc=1, device_id=(row, line_col(other(z, step))), device_id_type=pl.DeviceIdType.MESH)
    for step in range(ROWS):
        pl.semaphore_signal(barrier, inc=1, device_id=(other(row, step), mate), device_id_type=pl.DeviceIdType.MESH)

    sends = []

    def send(copy):
        copy.start()
        sends.append(copy)

    def sku_copy(side, step, there, slot):
        lanes = slice(side * half, (side + 1) * half)
        return remote(
            sku_ref.at[:, lanes], raw.at[slot, :, lanes], sku_sent.at[side, step], sku_landed.at[side, slot], there, col
        )

    pl.semaphore_wait(barrier, 2 * ROWS + LINE - 2)

    for step in (2, 3, 1):
        send(sku_copy(0, step, other(row, step), row))
    loads[1].wait()
    for piece in range(ROWS):
        probe_stage[piece * columns : (piece + 1) * columns, :] = probe_ref[
            :, piece * fold : (piece + 1) * fold
        ].astype(jnp.float32)
    probe_raw[row] = probe_stage[...].astype(jnp.bfloat16)
    for step in (2, 3, 1):
        there = other(row, step)
        send(remote(probe_raw.at[row], probe_raw.at[row], probe_sent.at[step], probe_landed.at[row], there, col))
    for step in (2, 3, 1):
        send(sku_copy(1, step, other(row, step), row))
    loads[0].wait()
    wide = strip_ref[...].astype(jnp.float32)
    scale = lax.rsqrt(jnp.sum(wide * wide, axis=0, keepdims=True) + 1e-06)
    strips[z] = (wide * scale).astype(jnp.bfloat16)
    for step in range(1, LINE):
        there = line_col(other(z, step))
        send(remote(strips.at[z], strips.at[z], strip_sent.at[step], strip_landed.at[z], row, there))

    loads[3].wait()
    for step in range(1, ROWS):
        there = other(row, step)
        remote(
            probe_raw.at[there], probe_raw.at[there], probe_sent.at[step], probe_landed.at[there], there, col
        ).wait_recv()
    for there in range(ROWS):
        folded = probe_raw[there].astype(jnp.float32)
        for piece in range(ROWS):
            probe_wide[there * columns : (there + 1) * columns, piece * fold : (piece + 1) * fold] = folded[
                piece * columns : (piece + 1) * columns
            ]

    pair = remote(full.at[0, core], full.at[1, core], pair_sent, pair_landed, row, mate)
    relay = remote(full.at[1, core], full.at[1, core], twin_sent, twin_landed, twin, col)

    def strip_wait(place, step):
        remote(
            strips.at[place], strips.at[place], strip_sent.at[step], strip_landed.at[place], row, line_col(place)
        ).wait_recv()

    def image_blocks(tasks):
        steps = [(number, first) for number in range(len(tasks)) for first in range(0, half, CHUNK)]
        totals = [jnp.zeros((block, strips.shape[2]), jnp.float32) for _ in tasks]
        corr = affinity = None
        for turn in range(len(steps) + 2):
            corr_next = affinity_next = None
            if turn < len(steps):
                number, first = steps[turn]
                which, side, place = tasks[number]
                corr_next = jnp.dot(
                    units[which, side, first : first + CHUNK, :], strips[place], preferred_element_type=jnp.float32
                )
            if corr is not None:
                affinity_next = jnp.exp2(corr * LOG2_E).astype(jnp.bfloat16)
            if affinity is not None:
                number, first = steps[turn - 2]
                which, side, place = tasks[number]
                totals[number] = totals[number] + jnp.dot(
                    full[which, side, factors:, first : first + CHUNK], affinity, preferred_element_type=jnp.float32
                )
            corr, affinity = corr_next, affinity_next
        return totals

    def image_block(which, side, place):
        return image_blocks([(which, side, place)])[0]

    for side in range(2):
        for step in range(1, ROWS):
            there = other(row, step)
            sku_copy(side, step, there, there).wait_recv()
        lanes = slice(side * half, (side + 1) * half)
        wide = raw[:, :, lanes].reshape(factors, half).astype(jnp.float32)
        scale = lax.rsqrt(jnp.sum(wide * wide, axis=0, keepdims=True) + 1e-06)
        unit = (wide * scale).astype(jnp.bfloat16)
        full[0, side, 0:factors, :] = unit
        full[0, side, factors:, :] = probe_wide[:, lanes].astype(jnp.bfloat16)
        units[0, side] = unit.T

        @pl.when(core == side)
        def _():
            pair.start()

        if side == 0:
            partial[z] = image_block(0, 0, z)
            near = other(z, 1)
            strip_wait(near, 1)
            partial[near] = image_block(0, 0, near)
        else:
            for place, total in zip((z, near), image_blocks([(0, 1, z), (0, 1, near)])):
                partial[place] += total

    far = [other(z, step) for step in range(2, LINE)]
    for number, place in enumerate(far):
        strip_wait(place, number + 2)
    totals = image_blocks([(0, side, place) for place in far for side in range(2)])
    for number, place in enumerate(far):
        partial[place] = totals[2 * number] + totals[2 * number + 1]

    places = [other(z, step) for step in range(1, LINE)]
    pair.wait_recv()
    relay.start()
    units[1, core] = full[1, core, 0:factors, :].T

    for place, total in zip(places, image_blocks([(1, core, place) for place in places])):
        partial[place] += total

    last = 1 - core
    remote(full.at[1, last], full.at[1, last], twin_sent, twin_landed, twin, col).wait_recv()
    units[1, last] = full[1, last, 0:factors, :].T

    for place, total in zip(places, image_blocks([(1, last, place) for place in places])):
        partial[place] += total
    for step in (3, 2, 1):
        place = other(z, step)
        remote(
            partial.at[place], arrived.at[z], image_sent.at[step], image_landed.at[z], row, line_col(place)
        ).start()

    image = partial[z] + sum(image_blocks([(1, 0, z), (1, 1, z)]))
    for step in range(1, LINE):
        place = other(z, step)
        remote(
            partial.at[place], arrived.at[place], image_sent.at[step], image_landed.at[place], row, line_col(place)
        ).wait_recv()
        image = image + arrived[place]

    loads[2].wait()
    local = lax.dot_general(
        image * weight_ref[...], image, (((1,), (1,)), ((), ())),
        precision=lax.Precision.HIGHEST, preferred_element_type=jnp.float32,
    )
    gram_line[z] = jnp.zeros(gram_line.shape[1:], jnp.float32)
    gram_line[z, :, 0:block] = local
    for step in range(1, LINE):
        there = line_col(other(z, step))
        send(remote(gram_line.at[z], gram_line.at[z], line_sent.at[step], line_landed.at[z], row, there))
    for step in range(1, LINE):
        place = other(z, step)
        remote(
            gram_line.at[place], gram_line.at[place], line_sent.at[step], line_landed.at[place], row, line_col(place)
        ).wait_recv()
    mine = row * 2 + y
    gram_group[mine] = (gram_line[0] + gram_line[1]) + (gram_line[2] + gram_line[3])
    for step in range(1, GROUP):
        there_row, there_y = other(row, step // 2), (y + step % 2) % 2
        send(
            remote(
                gram_group.at[mine], gram_group.at[mine], group_sent.at[step], group_landed.at[mine],
                there_row, z * 2 + there_y,
            )
        )
    for step in range(1, GROUP):
        there_row, there_y = other(row, step // 2), (y + step % 2) % 2
        slot = there_row * 2 + there_y
        remote(
            gram_group.at[slot], gram_group.at[slot], group_sent.at[step], group_landed.at[slot],
            there_row, z * 2 + there_y,
        ).wait_recv()
    gram = gram_group[0]
    for slot in range(1, GROUP):
        gram = gram + gram_group[slot]

    lanes = 128
    rank = lax.broadcasted_iota(jnp.int32, (block, lanes), 0)
    pivots = [jnp.broadcast_to(gram[:, k : k + 1], (block, lanes)) for k in range(block)]
    pieces = [image[:, left : left + lanes] for left in range(0, image.shape[1], lanes)]
    diagonal = jnp.ones((block, lanes), jnp.float32)
    for k in range(block):
        pivot = pivots[k][k : k + 1, :]
        diagonal = jnp.where(rank == k, pivot, diagonal)
        if k < block - 1:
            factor = jnp.where(rank > k, pivots[k] * (1.0 / pivot), 0.0)
            for later in range(k + 1, block):
                pivots[later] = pivots[later] - factor * pivots[later][k : k + 1, :]
            pieces = [piece - factor * piece[k : k + 1, :] for piece in pieces]
    root = lax.rsqrt(diagonal)
    for number, piece in enumerate(pieces):
        out_ref[:, number * lanes : (number + 1) * lanes] = piece * root

    for copy in sends:
        copy.wait_send()
    pair.wait_send()
    relay.wait_send()
    for step in range(1, LINE):
        remote(partial.at[z], arrived.at[z], image_sent.at[step], image_landed.at[z], row, mate).wait_send()


def fused_per_device(strip_factors, sku_factors, probe, demand_weight):
    strip, factors = strip_factors.shape
    skus, part = sku_factors.shape
    columns = probe.shape[1]
    block = ROWS * columns
    bf16, f32 = jnp.bfloat16, jnp.float32
    dma = pltpu.SemaphoreType.DMA
    whole = pl.BlockSpec(memory_space=pltpu.VMEM)
    far = pl.BlockSpec(memory_space=pltpu.HBM)
    return pl.pallas_call(
        fused,
        out_shape=pltpu.VMEM((block, strip), f32),
        in_specs=[far] * 4,
        out_specs=whole,
        scratch_shapes=[
            pltpu.VMEM((factors, strip), bf16),
            pltpu.VMEM((columns, skus), bf16),
            pltpu.VMEM((1, strip), f32),
            pltpu.VMEM((ROWS, part, skus), bf16),
            pltpu.VMEM((ROWS, block, skus // ROWS), bf16),
            pltpu.VMEM((block, skus // ROWS), f32),
            pltpu.VMEM((block, skus), f32),
            pltpu.VMEM((2, 2, factors + block, skus // 2), bf16),
            pltpu.VMEM((2, 2, skus // 2, factors), bf16),
            pltpu.VMEM((LINE, factors, strip), bf16),
            pltpu.VMEM((LINE, block, strip), f32),
            pltpu.VMEM((LINE, block, strip), f32),
            pltpu.VMEM((LINE, block, 128), f32),
            pltpu.VMEM((GROUP, block, 128), f32),
        ]
        + [dma((2, ROWS))] * 2 + [dma((ROWS,))] * 2 + [dma((LINE,))] * 2 + [dma] * 4 + [dma((LINE,))] * 4 + [dma((GROUP,))] * 2 + [dma((4,))],
        compiler_params=pltpu.CompilerParams(
            collective_id=0, has_side_effects=True, vmem_limit_bytes=60 * 1024 * 1024
        ),
        cost_estimate=pl.CostEstimate(
            flops=2 * LINE * strip * 2 * skus * (factors + block),
            bytes_accessed=2 * (strip * factors + skus * part + skus * columns) + 4 * block * strip,
            transcendentals=LINE * strip * 2 * skus,
        ),
    )(strip_factors.T, sku_factors.T, probe.T, demand_weight)


def fits(mesh):
    return mesh.shape["row"] == ROWS and mesh.shape["col"] == 2 * LINE


def solution(mesh):
    placed = (P(("row", "col"), None), P("col", "row"), P("col", "row"), P(None, ("row", "col")))
    plan = fused_per_device if fits(mesh) else per_device
    return jax.shard_map(
        plan, mesh=mesh, in_specs=placed, out_specs=P(None, ("row", "col")), check_vma=False
    )
```
